256 devices in a mesh: dp: 32 (over z, x), tensor: 8 (over y, core).
Axes of the slice: x: 4, y: 4, z: 8, core: 2. Of those that a mesh axis runs over, the one named last changes fastest.
Arguments:
- query: bfloat16 [256, 5120], P('dp', 'tensor'), may hold values from -256 to 256
- cache: bfloat16 [256, 2, 1024, 1024], P('dp', None, None, 'tensor'), may hold values from -6.5 to 6.5
- new_kv: bfloat16 [256, 2, 1024], P('dp', None, 'tensor'), may hold values from -12 to 12
- lengths: int32 [256], replicated, may hold values from 128 to 1024, as said below
- hidden_in: bfloat16 [256, 5120], P(None, 'dp'), may hold values from -24 to 24
- out_proj: bfloat16 [5120, 5120], P('tensor', 'dp'), may hold values from -0.078125 to 0.078125
- final_gain: float32 [5120], P('dp'), may hold values from 0.1 to 1.9
- lm_head: bfloat16 [152064, 5120], P(('dp', 'tensor')), may hold values from -32 to 32
- tokens: int32 [256], replicated, may hold values from 0 to 152063
- mu: float32 [256], replicated, may hold values from 6 to 10
Outputs:
- logprobs: float32 [256, 152064], P(None, ('dp', 'tensor'))
- surprise: float32 [256], replicated
- mu_next: float32 [256], replicated
The draws below stay inside these ranges and needn't reach their ends.
Inputs may be any that keep to these rules, and one draw needn't show every extreme that they name: Request r's cache holds live keys and values at positions 0 to lengths[r] - 1; the new token comes after them.
All inputs are finite; a program needn't handle non-finite values.
Results may differ from the reference program's by a relative error of at most 0.01.
Values may be sent and summed in bfloat16 or wider, within the bound.
No kernel may reach another device: no remote copies, remote signals or barrier semaphores. Data moves between devices by JAX's collectives and lax.ppermute only.
A program may use at most 64 MiB of HBM per device.

```python
import math
import jax
import jax.numpy as jnp
from jax import lax

D = 5120
HEADS = 40
KV_HEADS = 8
HEAD_DIM = 128
VOCAB = 152064
REQ_DEV = 8
MAXLEN = 1024
MINLEN = 128
REQUESTS = 256


def first_keys(key):
    return jnp.clip(jax.random.normal(key, (REQUESTS, KV_HEADS * HEAD_DIM), jnp.float32), -6.0, 6.0)


def draw_cache(key, part):
    leading = first_keys(key)
    key = jax.random.fold_in(key, 5)
    key_main = jax.random.fold_in(key, 0)
    slots = jnp.clip(jax.random.normal(key_main, (REQUESTS, 2, MAXLEN, KV_HEADS * HEAD_DIM), jnp.float32), -6.0, 6.0)
    slots = slots.at[:, 0, 0, :].set(leading)
    return slots.astype(jnp.bfloat16)


def draw_query(key, part):
    key = jax.random.fold_in(key, 7)
    key_main = jax.random.fold_in(key, 0)
    cached_value_rows = 2.0 * jnp.clip(jax.random.normal(key_main, (REQUESTS, HEADS * HEAD_DIM), jnp.float32), -6.0, 6.0)
    return cached_value_rows.astype(jnp.bfloat16)


def draw_lengths(key, part):
    key = jax.random.fold_in(key, 11)
    key_rank, key_fill = jax.random.split(key)
    groups = REQUESTS // REQ_DEV
    ranking = jax.random.permutation(key_rank, groups)
    ceiling = MINLEN + (MAXLEN - MINLEN) * (ranking + 1) // groups
    filled = jax.random.randint(key_fill, (groups, REQ_DEV), MINLEN, ceiling[:, None] + 1)
    filled = filled.at[:, 0].set(jnp.where(ranking == groups - 1, MAXLEN, filled[:, 0]))
    filled = filled.at[:, 1].set(jnp.where(ranking == 0, MINLEN, filled[:, 1]))
    return filled.reshape(REQUESTS).astype(jnp.int32)


def draw_hidden_in(key, part):
    key = jax.random.fold_in(key, 9)
    key_row, key_value = jax.random.split(key, 2)
    column = jnp.exp(math.log(3.0) * jnp.arange(D, dtype=jnp.float32) / D)
    row_scale = jnp.exp(jax.random.uniform(key_row, (REQUESTS,), jnp.float32, math.log(0.3), math.log(3.0)))
    cached_value_rows = jnp.clip(jax.random.normal(key_value, (REQUESTS, D), jnp.float32), -6.0, 6.0)
    return (0.15 * row_scale[:, None] * column[None, :] * cached_value_rows).astype(jnp.bfloat16)


def draw_lm_head(key, part):
    key = jax.random.fold_in(key, 13)
    key_spread, key_value = jax.random.split(key, 2)
    rising = jnp.exp(math.log(3.0) * jnp.arange(VOCAB, dtype=jnp.float32) / VOCAB)
    spread = jnp.exp(jax.random.uniform(key_spread, (VOCAB,), jnp.float32, 0.0, math.log(3.0)))
    row_scale = D ** (-0.5) * rising * spread
    cached_value_rows = jnp.clip(jax.random.normal(key_value, (VOCAB, D), jnp.float32), -6.0, 6.0)
    attention_weights = row_scale[:, None] * cached_value_rows
    return attention_weights.astype(jnp.bfloat16)


def with_ends(values, rng, low, top_value):
    dims = values.shape
    index_at = [jax.random.randint(jax.random.fold_in(rng, axis), (), 0, dims[axis]) for axis in range(len(dims))]
    values = values.at[tuple(index_at)].set(low)
    longest = dims.index(max(dims))
    index_at[longest] = (index_at[longest] + 1) % dims[longest]
    return values.at[tuple(index_at)].set(top_value)


def shard_levels(key, extent, cuts, least, high):
    level = 1.0
    for dim, shards_of in cuts:
        steps = jax.random.uniform(jax.random.fold_in(jax.random.fold_in(key, 6), dim), (shards_of,), jnp.float32, least / len(cuts), high / len(cuts))
        level = level * jnp.repeat(jnp.exp(steps), extent[dim] // shards_of).reshape((-1,) + (1,) * (len(extent) - 1 - dim))
    return level


def bell_draw(key, extent, scale, bound, cuts=(), held_as=jnp.bfloat16):
    values = jax.random.normal(key, extent, jnp.float32) * scale
    if len(cuts) > 0:
        values = shard_levels(key, extent, cuts, -0.22, 0.18) * values
    return jnp.clip(values, min=-bound, max=bound).astype(held_as)


def setup_inputs(seed: int = 0) -> dict:
    arg_keys = jax.random.split(jax.random.key(seed), 11)
    return {
        "query": draw_query(jax.random.fold_in(arg_keys[10], 71), 0),
        "cache": draw_cache(jax.random.fold_in(arg_keys[10], 71), 0),
        "new_kv": bell_draw(arg_keys[2], (REQUESTS, 2, KV_HEADS * HEAD_DIM), 3.0, 12.0, ((0, 32), (2, 8))),
        "lengths": draw_lengths(jax.random.fold_in(arg_keys[10], 71), 0),
        "hidden_in": draw_hidden_in(jax.random.fold_in(arg_keys[10], 71), 0),
        "out_proj": bell_draw(arg_keys[5], (HEADS * HEAD_DIM, D), (HEADS * HEAD_DIM) ** -0.5, 0.078125, ((0, 8), (1, 32))),
        "final_gain": jnp.clip(1.0 + 0.18 * jax.random.normal(arg_keys[6], (D,), jnp.float32), 0.1, 1.9),
        "lm_head": draw_lm_head(jax.random.fold_in(arg_keys[10], 71), 0),
        "tokens": with_ends(jax.random.randint(arg_keys[8], (REQUESTS,), 0, VOCAB), jax.random.fold_in(arg_keys[8], 1), 0, VOCAB - 1).astype(jnp.int32),
        "mu": jnp.clip(jax.random.uniform(arg_keys[9], (REQUESTS,), jnp.float32, 6.0, 10.0), 6.0, 10.0),
    }


masked_score = -1e+30
epsilon = 1e-06
learn_rate = 0.1
target_bits = 5.0

def reference(query, cache, new_kv, lengths, hidden_in, out_proj, final_gain, lm_head, tokens, mu):
    group_size = HEADS // KV_HEADS
    attention_scale = HEAD_DIM ** (-0.5)
    positions = jnp.arange(MAXLEN, dtype=jnp.int32)

    def one_request(items):
        query_row, slots, fresh, live = items
        per_head_rows = query_row.astype(jnp.float32).reshape(KV_HEADS, group_size, HEAD_DIM)
        cached_key_rows = slots[0].astype(jnp.float32).reshape(MAXLEN, KV_HEADS, HEAD_DIM)
        cached_value_rows = slots[1].astype(jnp.float32).reshape(MAXLEN, KV_HEADS, HEAD_DIM)
        new_key = fresh[0].astype(jnp.float32).reshape(KV_HEADS, HEAD_DIM)
        new_value = fresh[1].astype(jnp.float32).reshape(KV_HEADS, HEAD_DIM)
        attention_scores = jnp.einsum('wzh,awh->wza', per_head_rows, cached_key_rows, precision=lax.Precision.HIGHEST) * attention_scale
        attention_scores = jnp.where(positions < live, attention_scores, masked_score)
        own_score = jnp.einsum('kgd,kd->kg', per_head_rows, new_key, precision=lax.Precision.HIGHEST) * attention_scale
        top_score = jnp.maximum(lax.optimization_barrier(jnp.max(attention_scores, axis=-1)), own_score)
        attention_weights = jnp.exp(attention_scores - top_score[..., None])
        own_weight = jnp.exp(own_score - top_score)
        weight_mass = lax.optimization_barrier(jnp.sum(attention_weights, axis=-1)) + own_weight
        weighted_value_sum = jnp.einsum('hqi,ihz->hqz', attention_weights, cached_value_rows, precision=lax.Precision.HIGHEST)
        weighted_value_sum = weighted_value_sum + own_weight[..., None] * new_value[:, None, :]
        return (weighted_value_sum / weight_mass[..., None]).reshape(HEADS * HEAD_DIM).astype(jnp.bfloat16)
    attended = lax.map(one_request, (query, cache, new_kv, lengths))
    projected = jnp.dot(attended, out_proj, preferred_element_type=jnp.float32)
    resid = (hidden_in.astype(jnp.float32) + projected).astype(jnp.bfloat16)
    resid_wide = resid.astype(jnp.float32)
    meansq = lax.optimization_barrier(jnp.sum(resid_wide * resid_wide, axis=1)) / D
    normed = (resid_wide * lax.rsqrt(meansq + epsilon)[:, None] * final_gain[None, :]).astype(jnp.bfloat16)
    logits = lax.dot_general(normed, lm_head, (((1,), (1,)), ((), ())), preferred_element_type=jnp.float32)
    top_logit = lax.optimization_barrier(jnp.max(logits, axis=1))
    log_mass = top_logit + jnp.log(lax.optimization_barrier(jnp.sum(jnp.exp(logits - top_logit[:, None]), axis=1)))
    logprobs = logits - log_mass[:, None]
    chosen = jnp.take_along_axis(logits, tokens[:, None].astype(jnp.int32), axis=1)[:, 0]
    surprise = (log_mass - chosen) / math.log(2.0)
    mu_next = mu - learn_rate * (surprise - target_bits)
    return (logprobs, surprise, mu_next)
```

```python
import math

import jax
import jax.numpy as jnp
import numpy as np
from jax import lax
from jax.sharding import Mesh
from jax.sharding import PartitionSpec as P

D = 5120
HEADS = 40
KV_HEADS = 8
HEAD_DIM = 128

masked_score = -1e30
epsilon = 1e-06
learn_rate = 0.1
target_bits = 5.0

bf16 = jnp.bfloat16
f32 = jnp.float32


def attend_all(query, cache, new_kv, own_lengths):
    request_count = query.shape[0]
    kv_local = cache.shape[3] // HEAD_DIM
    group_size = HEADS // KV_HEADS
    slots = cache.shape[2]
    per_head_rows = query.reshape(request_count, kv_local, group_size, HEAD_DIM)
    new_keys = new_kv[:, 0].reshape(request_count, kv_local, HEAD_DIM)
    new_values = new_kv[:, 1].reshape(request_count, kv_local, HEAD_DIM).astype(f32)
    scale = HEAD_DIM ** (-0.5)
    own_score = jnp.einsum("rkgd,rkd->rkg", per_head_rows, new_keys, preferred_element_type=f32) * scale
    keys = cache[:, 0].reshape(request_count, slots, kv_local, HEAD_DIM)
    values = cache[:, 1].reshape(request_count, slots, kv_local, HEAD_DIM)
    scores = jnp.einsum("rkgd,rbkd->rkgb", per_head_rows, keys, preferred_element_type=f32) * scale
    live = jnp.arange(slots, dtype=jnp.int32)[None, :] < own_lengths[:, None]
    scores = jnp.where(live[:, None, None, :], scores, masked_score)
    top = jnp.maximum(jnp.max(scores, axis=-1), own_score)
    weights = jnp.exp(scores - top[..., None])
    own_weight = jnp.exp(own_score - top)
    mass = jnp.sum(weights, axis=-1) + own_weight
    total = jnp.einsum(
        "rkgb,rbkd->rkgd", weights, values.astype(f32), precision=lax.Precision.HIGHEST
    )
    total = total + own_weight[..., None] * new_values[:, :, None, :]
    return (total / mass[..., None]).reshape(request_count, -1).astype(bf16)


def spread(block, axes, count):
    many = jnp.broadcast_to(block[None], (count,) + block.shape)
    return lax.all_to_all(many, axes, split_axis=0, concat_axis=0, tiled=False)


def three_parts(wide):
    first = wide.astype(bf16)
    rest = wide - first.astype(f32)
    second = rest.astype(bf16)
    third = (rest - second.astype(f32)).astype(bf16)
    return first, second, third


def shards(query, cache, new_kv, lengths, hidden_in, out_proj, final_gain, lm_head, tokens, mu):
    nz, nx, ny, nc = (lax.axis_size(a) for a in ("z", "x", "y", "c"))
    z, x, y, c = (lax.axis_index(a) for a in ("z", "x", "y", "c"))
    request_count = query.shape[0]
    columns = out_proj.shape[1]
    part = c * ny + y

    gain_rows = jnp.stack(three_parts(final_gain))
    packs = []
    for step in range(nx):
        target = lax.rem(x + step, nx)
        rows = lax.dynamic_slice_in_dim(hidden_in, (part * nx + target) * request_count, request_count)
        pack = jnp.concatenate([out_proj, rows, gain_rows], axis=0)
        if step:
            pack = lax.ppermute(pack, "x", [(i, (i + step) % nx) for i in range(nx)])
        packs.append(pack)
    heads = out_proj.shape[0]
    table = jnp.concatenate([p[:heads] for p in packs], axis=1)
    hidden = jnp.concatenate([p[heads : heads + request_count] for p in packs], axis=1)
    gains = jnp.concatenate([p[heads + request_count :] for p in packs], axis=1)

    own_lengths = lax.dynamic_slice_in_dim(lengths, (z * nx + x) * request_count, request_count)
    attended = attend_all(query, cache, new_kv, own_lengths)
    gathered = spread(attended, "z", nz).reshape(nz * request_count, -1)
    partial = jnp.dot(gathered, table, preferred_element_type=f32)
    partial = partial.reshape(nz, request_count, nx * columns)
    partial = lax.all_to_all(partial, ("c", "y"), split_axis=0, concat_axis=0, tiled=False)
    resid = (hidden.astype(f32) + jnp.sum(partial, axis=0)).astype(bf16)

    both = jnp.concatenate([resid, gains], axis=0)
    blocks = [both[:, i * columns : (i + 1) * columns] for i in range(nx)]
    twice = jnp.concatenate(blocks[::-1] + blocks[::-1], axis=1)
    ordered = lax.dynamic_slice_in_dim(twice, (nx - 1 - x) * columns, nx * columns, axis=1)

    rows = spread(ordered, "z", nz)
    gain = jnp.sum(rows[:, request_count:].astype(f32), axis=1)
    resid_wide = rows[:, :request_count].astype(f32)
    sum_squares = jnp.sum(resid_wide * resid_wide, axis=(0, 2))
    factor = lax.rsqrt(sum_squares / D + epsilon)
    normed = (resid_wide * factor[None, :, None] * gain[:, None, :]).astype(bf16)
    normed = jnp.swapaxes(normed, 0, 1).reshape(request_count, -1)

    half = spread(normed, ("y", "x"), ny * nx).reshape(ny * nx * request_count, -1)
    other = lax.ppermute(half, "c", [(i, 1 - i) for i in range(2)])
    first = jnp.where(c == 0, half, other)
    second = jnp.where(c == 0, other, half)
    everyone = jnp.concatenate([first, second], axis=0)
    logits = lax.dot_general(lm_head, everyone, (((1,), (1,)), ((), ())), preferred_element_type=f32)

    vocab_rows = lm_head.shape[0]
    offset = (((z * nx + x) * ny + y) * nc + c) * vocab_rows
    hits = jnp.arange(vocab_rows, dtype=jnp.int32)[:, None] == (tokens - offset)[None, :]
    picked = jnp.sum(jnp.where(hits, logits, 0.0), axis=0)
    top = jnp.max(logits, axis=0)
    log_mass = top + jnp.log(jnp.sum(jnp.exp(logits - top[None, :]), axis=0))
    for axes, count in ((("x", "y", "c"), nx * ny * nc), ("z", nz)):
        stats = spread(jnp.stack([log_mass, picked]), axes, count)
        top = jnp.max(stats[:, 0], axis=0)
        log_mass = top + jnp.log(jnp.sum(jnp.exp(stats[:, 0] - top[None, :]), axis=0))
        picked = jnp.sum(stats[:, 1], axis=0)
    logprobs = (logits - log_mass[None, :]).T
    surprise = (log_mass - picked) / math.log(2.0)
    mu_next = mu - learn_rate * (surprise - target_bits)
    return (logprobs, surprise, mu_next)


def solution(mesh):
    grid = Mesh(np.asarray(mesh.devices).reshape(8, 4, 4, 2), ("z", "x", "y", "c"))
    dp, tensor = ("z", "x"), ("y", "c")
    placed = (
        P(dp, tensor),
        P(dp, None, None, tensor),
        P(dp, None, tensor),
        P(),
        P(None, dp),
        P(tensor, dp),
        P(dp),
        P(dp + tensor, None),
        P(),
        P(),
    )
    return jax.shard_map(
        shards,
        mesh=grid,
        in_specs=placed,
        out_specs=(P(None, dp + tensor), P(), P()),
        check_vma=False,
    )
```

```python
import functools
import math

import jax
import jax.numpy as jnp
import numpy as np
from jax import lax
from jax.experimental import pallas as pl
from jax.experimental.pallas import tpu as pltpu
from jax.sharding import Mesh
from jax.sharding import PartitionSpec as P

D = 5120
HEADS = 40
KV_HEADS = 8
HEAD_DIM = 128

masked_score = -1e30
epsilon = 1e-06
learn_rate = 0.1
target_bits = 5.0

bf16 = jnp.bfloat16
f32 = jnp.float32
LANES = 128

IN_VMEM = pl.BlockSpec(memory_space=pltpu.VMEM)
IN_SMEM = pl.BlockSpec(memory_space=pltpu.SMEM)
IN_PLACE = pl.BlockSpec(memory_space=pl.ANY)
SMALL = pltpu.CompilerParams(vmem_limit_bytes=20 << 20)
WIDE = pltpu.CompilerParams(vmem_limit_bytes=50 << 20)
WHOLE = pltpu.CompilerParams(vmem_limit_bytes=60 << 20)
TAIL = 16
CHUNK = 1280


def three_parts(wide):
    first = wide.astype(bf16).astype(f32)
    rest = wide - first
    second = rest.astype(bf16).astype(f32)
    third = (rest - second).astype(bf16).astype(f32)
    return first, second, third


def pack_kernel(count, place_ref, table_hbm, hidden_hbm, gain_hbm, own_ref, *refs):
    packs, (table_ref, hidden_ref, gain_ref, sems) = refs[:-4], refs[-4:]
    loads = [
        pltpu.make_async_copy(source, target, sems.at[k])
        for k, (source, target) in enumerate(
            ((table_hbm, table_ref), (hidden_hbm, hidden_ref), (gain_hbm, gain_ref))
        )
    ]
    for load in loads:
        load.start()
    columns, heads = table_ref.shape
    requests = hidden_ref.shape[1]
    for load in loads:
        load.wait()
    row = lax.broadcasted_iota(jnp.int32, (count, requests), 0)
    lane = lax.broadcasted_iota(jnp.int32, (count, requests), 1)
    parts = three_parts(gain_ref[...])
    below = jnp.concatenate(parts + (jnp.zeros((TAIL - count - 3, columns), f32),), axis=0)
    for step in range(len(packs) + 1):
        chosen = jnp.where(lane == row + place_ref[step], 1.0, 0.0).astype(bf16)
        hidden = lax.dot_general(
            chosen, hidden_ref[...], (((1,), (1,)), ((), ())), preferred_element_type=f32
        )
        tail = jnp.concatenate([hidden, below], axis=0).astype(bf16)
        if step == 0:
            own_ref[...] = tail
        else:
            packs[step - 1][:columns] = table_ref[...]
            packs[step - 1][columns:] = jnp.zeros((TAIL, heads), bf16)
            packs[step - 1][columns:, :columns] = tail


def attend_kernel(group, base_ref, lengths_ref, query_ref, new_ref, cache_ref, out_ref, slots_ref, rows_ref, sems):
    count, _, slots, head_dim = cache_ref.shape
    copies = out_ref.shape[0]
    scale = head_dim ** (-0.5)
    loads = [pltpu.make_async_copy(cache_ref.at[r], slots_ref.at[r], sems.at[r]) for r in range(count)]
    for load in loads:
        load.start()
    query = query_ref[...].astype(f32)
    fresh = new_ref[...].astype(f32)
    position = lax.broadcasted_iota(jnp.int32, (8, slots), 1)
    for r in range(count):
        pieces = [query[r : r + 1, g * head_dim : (g + 1) * head_dim] for g in range(group)]
        pieces.append(jnp.zeros((8 - group, head_dim), f32))
        heads = jnp.concatenate(pieces, axis=0)
        own_score = jnp.sum(heads * fresh[r, 0:1], axis=1, keepdims=True) * scale
        loads[r].wait()
        scores = lax.dot_general(
            heads.astype(bf16), slots_ref[r, 0], (((1,), (1,)), ((), ())), preferred_element_type=f32
        ) * scale
        scores = jnp.where(position < lengths_ref[base_ref[0] + r], scores, masked_score)
        top = jnp.maximum(jnp.max(scores, axis=1, keepdims=True), own_score)
        weights = jnp.exp(scores - top)
        own_weight = jnp.exp(own_score - top)
        mass = jnp.sum(weights, axis=1, keepdims=True) + own_weight
        stacked = jnp.concatenate(three_parts(weights), axis=0).astype(bf16)
        sums = jnp.dot(stacked, slots_ref[r, 1], preferred_element_type=f32)
        total = sums[:8] + sums[8:16] + sums[16:24] + own_weight * fresh[r, 1:2]
        total = total / mass
        for g in range(group):
            rows_ref[r : r + 1, g * head_dim : (g + 1) * head_dim] = total[g : g + 1]
    done = rows_ref[...].astype(bf16)
    for k in range(copies):
        out_ref[k] = done


def resid_kernel(x_ref, partial_ref, own_ref, *refs):
    packs, out_ref = refs[:-1], refs[-1]
    count, width = partial_ref.shape[1:]
    columns = width // (len(packs) + 1)
    total = partial_ref[0]
    for k in range(1, partial_ref.shape[0]):
        total = total + partial_ref[k]
    squares = jnp.zeros((count, 1), f32)
    blocks = []
    for step in range(len(packs) + 1):
        tail = own_ref[...] if step == 0 else packs[step - 1][columns:, :columns]
        tail = tail.astype(f32)
        gain = tail[count : count + 1] + tail[count + 1 : count + 2] + tail[count + 2 : count + 3]
        resid = total[:, step * columns : (step + 1) * columns] + tail[:count]
        resid = resid.astype(bf16).astype(f32)
        squares = squares + jnp.sum(resid * resid, axis=1, keepdims=True)
        blocks.append(resid * gain)
    ordered = pltpu.roll(jnp.concatenate(blocks[::-1], axis=1), x_ref[0], 1)
    lane = lax.broadcasted_iota(jnp.int32, (count, LANES), 1)
    spare = jnp.zeros((count, LANES), f32)
    for k, part in enumerate(three_parts(squares)):
        spare = jnp.where(lane == k, part, spare)
    done = jnp.concatenate([ordered, spare], axis=1).astype(bf16)
    for k in range(out_ref.shape[0]):
        out_ref[k] = done


def norm_kernel(rows_ref, out_ref):
    blocks, count, padded = rows_ref.shape
    width = padded - LANES
    squares = jnp.zeros((count, LANES), f32)
    for k in range(blocks):
        squares = squares + rows_ref[k, :, width:].astype(f32)
    factor = lax.rsqrt(jnp.sum(squares, axis=1, keepdims=True) / D + epsilon)
    for k in range(blocks):
        done = (rows_ref[k, :, :width].astype(f32) * factor).astype(bf16)
        for copy in range(out_ref.shape[0]):
            out_ref[copy, :, k * width : (k + 1) * width] = done


def logits_kernel(head_hbm, rows_ref, ids_ref, logits_ref, stats_ref, head_ref, sems):
    depth = head_ref.shape[1]
    spans = [slice(k, k + CHUNK) for k in range(0, depth, CHUNK)]
    loads = [
        pltpu.make_async_copy(head_hbm.at[:, span], head_ref.at[:, span], sems.at[k])
        for k, span in enumerate(spans)
    ]
    for load in loads:
        load.start()
    for k, span in enumerate(spans):
        loads[k].wait()
        product = lax.dot_general(
            head_ref[:, span], rows_ref[:, span], (((1,), (1,)), ((), ())), preferred_element_type=f32
        )
        if k == 0:
            logits_ref[...] = product
        else:
            logits_ref[...] += product
    logits = logits_ref[...]
    top = jnp.max(logits, axis=0, keepdims=True)
    log_mass = top + jnp.log(jnp.sum(jnp.exp(logits - top), axis=0, keepdims=True))
    hits = lax.broadcasted_iota(jnp.int32, logits.shape, 0) == ids_ref[...]
    picked = jnp.sum(jnp.where(hits, logits, 0.0), axis=0, keepdims=True)
    stats_ref[...] = jnp.concatenate([log_mass, picked], axis=0)


def final_kernel(logits_ref, stats_ref, mu_ref, logprobs_ref, surprise_ref, mu_next_ref):
    masses = stats_ref[:, 0]
    top = jnp.max(masses, axis=0, keepdims=True)
    log_mass = top + jnp.log(jnp.sum(jnp.exp(masses - top), axis=0, keepdims=True))
    picked = jnp.sum(stats_ref[:, 1], axis=0, keepdims=True)
    logprobs_ref[...] = logits_ref[...] - log_mass
    surprise = (log_mass - picked) / math.log(2.0)
    surprise_ref[...] = surprise
    mu_next_ref[...] = mu_ref[...] - learn_rate * (surprise - target_bits)


def spread(block, axes, count):
    many = jnp.broadcast_to(block[None], (count,) + block.shape)
    return lax.all_to_all(many, axes, split_axis=0, concat_axis=0, tiled=False)


def shards(query, cache, new_kv, lengths, hidden_in, out_proj, final_gain, lm_head, tokens, mu):
    nz, nx, ny, nc = (lax.axis_size(a) for a in ("z", "x", "y", "c"))
    z, x, y, c = (lax.axis_index(a) for a in ("z", "x", "y", "c"))
    count = query.shape[0]
    heads, columns = out_proj.shape
    part = c * ny + y

    targets = lax.rem(x + jnp.arange(nx, dtype=jnp.int32), nx)
    place = (part * nx + targets) * count
    pack_shape = jax.ShapeDtypeStruct((columns + TAIL, heads), bf16)
    own_tail, *packs = pl.pallas_call(
        functools.partial(pack_kernel, count),
        out_shape=[jax.ShapeDtypeStruct((TAIL, columns), bf16)] + [pack_shape] * (nx - 1),
        in_specs=[IN_SMEM] + [IN_PLACE] * 3,
        out_specs=[IN_VMEM] * nx,
        scratch_shapes=[
            pltpu.VMEM((columns, heads), bf16),
            pltpu.VMEM((columns, hidden_in.shape[0]), bf16),
            pltpu.VMEM((1, columns), f32),
            pltpu.SemaphoreType.DMA((3,)),
        ],
        compiler_params=WHOLE,
        name="pack",
    )(place, out_proj.T, hidden_in.T, final_gain[None])
    packs = [
        lax.ppermute(pack, "x", [(i, (i + step) % nx) for i in range(nx)])
        for step, pack in enumerate(packs, 1)
    ]
    table = jnp.concatenate([out_proj.T] + [p[:columns] for p in packs], axis=0)

    many = pl.pallas_call(
        functools.partial(attend_kernel, HEADS // KV_HEADS),
        out_shape=jax.ShapeDtypeStruct((nz,) + query.shape, bf16),
        in_specs=[IN_SMEM] * 2 + [IN_VMEM] * 2 + [IN_PLACE],
        out_specs=IN_VMEM,
        scratch_shapes=[
            pltpu.VMEM(cache.shape, bf16),
            pltpu.VMEM(query.shape, f32),
            pltpu.SemaphoreType.DMA((count,)),
        ],
        compiler_params=WHOLE,
        name="attend",
    )(((z * nx + x) * count)[None], lengths, query, new_kv, cache)
    gathered = lax.all_to_all(many, "z", split_axis=0, concat_axis=0, tiled=False)
    gathered = gathered.reshape(nz * count, -1)
    partial = lax.dot_general(
        gathered, table, (((1,), (1,)), ((), ())), preferred_element_type=f32
    )
    partial = partial.reshape(nz, count, nx * columns)
    partial = lax.all_to_all(partial, ("c", "y"), split_axis=0, concat_axis=0, tiled=False)

    width = nx * columns
    rows = pl.pallas_call(
        resid_kernel,
        out_shape=jax.ShapeDtypeStruct((nz, count, width + LANES), bf16),
        in_specs=[IN_SMEM] + [IN_VMEM] * (nx + 1),
        out_specs=IN_VMEM,
        compiler_params=SMALL,
        name="resid",
    )((lax.rem(x + 1, nx) * columns)[None], partial, own_tail, *packs)
    rows = lax.all_to_all(rows, "z", split_axis=0, concat_axis=0, tiled=False)
    half = pl.pallas_call(
        norm_kernel,
        out_shape=jax.ShapeDtypeStruct((nx * ny, count, nz * width), bf16),
        in_specs=[IN_VMEM],
        out_specs=IN_VMEM,
        compiler_params=SMALL,
        name="norm",
    )(rows)
    half = lax.all_to_all(half, ("x", "y"), split_axis=0, concat_axis=0, tiled=False)
    other = lax.ppermute(half, "c", [(i, 1 - i) for i in range(2)])
    half, other = (
        jnp.swapaxes(h.reshape(nx, ny, count, -1), 0, 1).reshape(nx * ny * count, -1) for h in (half, other)
    )
    first = jnp.where(c == 0, half, other)
    second = jnp.where(c == 0, other, half)
    everyone = jnp.concatenate([first, second], axis=0)

    vocab = lm_head.shape[0]
    requests = everyone.shape[0]
    offset = (((z * nx + x) * ny + y) * nc + c) * vocab
    logits, stats = pl.pallas_call(
        logits_kernel,
        out_shape=[jax.ShapeDtypeStruct((vocab, requests), f32), jax.ShapeDtypeStruct((2, requests), f32)],
        in_specs=[IN_PLACE] + [IN_VMEM] * 2,
        out_specs=[IN_VMEM] * 2,
        scratch_shapes=[
            pltpu.VMEM(lm_head.shape, bf16),
            pltpu.SemaphoreType.DMA((lm_head.shape[1] // CHUNK,)),
        ],
        compiler_params=WIDE,
        name="logits",
    )(lm_head, everyone, (tokens - offset)[None])

    stats = spread(stats, ("x", "y", "c"), nx * ny * nc)
    top = jnp.max(stats[:, 0], axis=0)
    log_mass = top + jnp.log(jnp.sum(jnp.exp(stats[:, 0] - top[None, :]), axis=0))
    picked = jnp.sum(stats[:, 1], axis=0)
    stats = spread(jnp.stack([log_mass, picked]), "z", nz)
    row_shape = jax.ShapeDtypeStruct((1, requests), f32)
    logprobs, surprise, mu_next = pl.pallas_call(
        final_kernel,
        out_shape=[jax.ShapeDtypeStruct((vocab, requests), f32), row_shape, row_shape],
        in_specs=[IN_VMEM] * 3,
        out_specs=[IN_VMEM] * 3,
        compiler_params=SMALL,
        name="final",
    )(logits, stats, mu[None])
    return (logprobs.T, surprise[0], mu_next[0])


def solution(mesh):
    grid = Mesh(np.asarray(mesh.devices).reshape(8, 4, 4, 2), ("z", "x", "y", "c"))
    dp, tensor = ("z", "x"), ("y", "c")
    placed = (
        P(dp, tensor),
        P(dp, None, None, tensor),
        P(dp, None, tensor),
        P(),
        P(None, dp),
        P(tensor, dp),
        P(dp),
        P(dp + tensor, None),
        P(),
        P(),
    )
    return jax.shard_map(
        shards,
        mesh=grid,
        in_specs=placed,
        out_specs=(P(None, dp + tensor), P(), P()),
        check_vma=False,
    )
```

```python
import functools
import math

import jax
import jax.numpy as jnp
import numpy as np
from jax import lax
from jax.experimental import pallas as pl
from jax.experimental.pallas import tpu as pltpu
from jax.sharding import Mesh
from jax.sharding import PartitionSpec as P

D = 5120
HEADS = 40
KV_HEADS = 8
HEAD_DIM = 128

masked_score = -1e30
epsilon = 1e-06
learn_rate = 0.1
target_bits = 5.0

bf16 = jnp.bfloat16
f32 = jnp.float32
LANES = 128

IN_VMEM = pl.BlockSpec(memory_space=pltpu.VMEM)
IN_SMEM = pl.BlockSpec(memory_space=pltpu.SMEM)
IN_PLACE = pl.BlockSpec(memory_space=pl.ANY)
SMALL = pltpu.CompilerParams(vmem_limit_bytes=20 << 20)
WIDE = pltpu.CompilerParams(vmem_limit_bytes=44 << 20)
WHOLE = pltpu.CompilerParams(vmem_limit_bytes=60 << 20)
TAIL = 16
CHUNK = 1280


def three_parts(wide):
    first = wide.astype(bf16).astype(f32)
    rest = wide - first
    second = rest.astype(bf16).astype(f32)
    third = (rest - second).astype(bf16).astype(f32)
    return first, second, third


def tails_of(count, part, x, hidden_ref, gain_ref, tail_refs):
    columns, requests = hidden_ref.shape
    row = lax.broadcasted_iota(jnp.int32, (count, requests), 0)
    lane = lax.broadcasted_iota(jnp.int32, (count, requests), 1)
    parts = three_parts(gain_ref[...])
    below = jnp.concatenate(parts + (jnp.zeros((TAIL - count - 3, columns), f32),), axis=0)
    for step, tail_ref in enumerate(tail_refs):
        target = lax.rem(x + step, len(tail_refs))
        place = (part * len(tail_refs) + target) * count
        chosen = jnp.where(lane == row + place, 1.0, 0.0).astype(bf16)
        hidden = lax.dot_general(
            chosen, hidden_ref[...], (((1,), (1,)), ((), ())), preferred_element_type=f32
        )
        tail_ref[...] = jnp.concatenate([hidden, below], axis=0).astype(bf16)


def attend_kernel(group, sizes, lengths_ref, query_ref, new_ref, hidden_ref, gain_ref, cache_ref, *refs):
    out_ref, tail_refs, (slots_ref, rows_ref, sums_ref, sems) = refs[0], refs[1:-4], refs[-4:]
    count, _, slots, head_dim = cache_ref.shape
    z, x, y, c = (lax.axis_index(a) for a in ("z", "x", "y", "c"))
    scale = head_dim ** (-0.5)
    loads = [
        [
            pltpu.make_async_copy(cache_ref.at[r, kind], slots_ref.at[r, kind], sems.at[kind, r])
            for r in range(count)
        ]
        for kind in range(2)
    ]
    for load in loads[0] + loads[1]:
        load.start()
    tails_of(count, c * sizes["y"] + y, x, hidden_ref, gain_ref, tail_refs)

    query = query_ref[...].astype(f32)
    fresh = new_ref[...].astype(f32)
    rows_ref[...] = jnp.zeros_like(rows_ref)
    for g in range(group):
        rows_ref[pl.ds(g, count, stride=8), :] = query[:, g * head_dim : (g + 1) * head_dim]
    heads = rows_ref[...]
    new_keys = jnp.concatenate([jnp.broadcast_to(fresh[r, 0:1], (8, head_dim)) for r in range(count)], axis=0)
    own_score = jnp.sum(heads * new_keys, axis=1, keepdims=True) * scale
    heads = heads.astype(bf16)
    position = lax.broadcasted_iota(jnp.int32, (8, slots), 1)
    base = (z * sizes["x"] + x) * count
    for load in loads[0]:
        load.wait()
    scores = []
    for r in range(count):
        score = lax.dot_general(
            heads[8 * r : 8 * r + 8],
            slots_ref[r, 0],
            (((1,), (1,)), ((), ())),
            preferred_element_type=f32,
        )
        scores.append(jnp.where(position < lengths_ref[base + r], score * scale, masked_score))
    scores = jnp.concatenate(scores, axis=0)
    top = jnp.maximum(jnp.max(scores, axis=1, keepdims=True), own_score)
    weights = jnp.exp(scores - top)
    own_weight = jnp.exp(own_score - top)
    mass = jnp.sum(weights, axis=1, keepdims=True) + own_weight
    parts = three_parts(weights)
    for load in loads[1]:
        load.wait()
    for r in range(count):
        span = slice(8 * r, 8 * r + 8)
        stacked = jnp.concatenate([part[span] for part in parts], axis=0).astype(bf16)
        sums = jnp.dot(stacked, slots_ref[r, 1], preferred_element_type=f32)
        total = sums[:8] + sums[8:16] + sums[16:24] + own_weight[span] * fresh[r, 1:2]
        sums_ref[span] = total / mass[span]
    done = jnp.concatenate([sums_ref[pl.ds(g, count, stride=8), :] for g in range(group)], axis=1).astype(bf16)
    for k in range(out_ref.shape[0]):
        out_ref[k] = done


def resid_kernel(partial_ref, *refs):
    tails, out_ref = refs[:-1], refs[-1]
    count, width = partial_ref.shape[1:]
    columns = width // len(tails)
    total = partial_ref[0]
    for k in range(1, partial_ref.shape[0]):
        total = total + partial_ref[k]
    squares = jnp.zeros((count, 1), f32)
    blocks = []
    for step, tail_ref in enumerate(tails):
        tail = tail_ref[...].astype(f32)
        gain = tail[count : count + 1] + tail[count + 1 : count + 2] + tail[count + 2 : count + 3]
        resid = total[:, step * columns : (step + 1) * columns] + tail[:count]
        resid = resid.astype(bf16).astype(f32)
        squares = squares + jnp.sum(resid * resid, axis=1, keepdims=True)
        blocks.append(resid * gain)
    shift = lax.rem(lax.axis_index("x") + 1, len(tails)) * columns
    ordered = pltpu.roll(jnp.concatenate(blocks[::-1], axis=1), shift, 1)
    lane = lax.broadcasted_iota(jnp.int32, (count, LANES), 1)
    spare = jnp.zeros((count, LANES), f32)
    for k, part in enumerate(three_parts(squares)):
        spare = jnp.where(lane == k, part, spare)
    done = jnp.concatenate([ordered, spare], axis=1).astype(bf16)
    for k in range(out_ref.shape[0]):
        out_ref[k] = done


def norm_kernel(rows_ref, out_ref):
    blocks, count, padded = rows_ref.shape
    width = padded - LANES
    squares = jnp.zeros((count, LANES), f32)
    for k in range(blocks):
        squares = squares + rows_ref[k, :, width:].astype(f32)
    factor = lax.rsqrt(jnp.sum(squares, axis=1, keepdims=True) / D + epsilon)
    for k in range(blocks):
        done = (rows_ref[k, :, :width].astype(f32) * factor).astype(bf16)
        for copy in range(out_ref.shape[0]):
            out_ref[copy, :, k * width : (k + 1) * width] = done


def fetch_kernel(head_hbm, after_ref, head_ref, sem):
    load = pltpu.make_async_copy(head_hbm, head_ref, sem)
    load.start()
    load.wait()


def logits_kernel(head_ref, rows_ref, ids_ref, logits_ref, stats_ref):
    depth = head_ref.shape[1]
    for k in range(depth // CHUNK):
        span = slice(k * CHUNK, (k + 1) * CHUNK)
        product = lax.dot_general(
            head_ref[:, span], rows_ref[:, span], (((1,), (1,)), ((), ())), preferred_element_type=f32
        )
        if k == 0:
            logits_ref[...] = product
        else:
            logits_ref[...] += product
    logits = logits_ref[...]
    top = jnp.max(logits, axis=0, keepdims=True)
    log_mass = top + jnp.log(jnp.sum(jnp.exp(logits - top), axis=0, keepdims=True))
    hits = lax.broadcasted_iota(jnp.int32, logits.shape, 0) == ids_ref[...]
    picked = jnp.sum(jnp.where(hits, logits, 0.0), axis=0, keepdims=True)
    stats_ref[...] = jnp.concatenate([log_mass, picked], axis=0)


def final_kernel(logits_ref, stats_ref, mu_ref, logprobs_ref, surprise_ref, mu_next_ref):
    masses = stats_ref[:, 0]
    top = jnp.max(masses, axis=0, keepdims=True)
    log_mass = top + jnp.log(jnp.sum(jnp.exp(masses - top), axis=0, keepdims=True))
    picked = jnp.sum(stats_ref[:, 1], axis=0, keepdims=True)
    logprobs_ref[...] = logits_ref[...] - log_mass
    surprise = (log_mass - picked) / math.log(2.0)
    surprise_ref[...] = surprise
    mu_next_ref[...] = mu_ref[...] - learn_rate * (surprise - target_bits)


def spread(block, axes, count):
    many = jnp.broadcast_to(block[None], (count,) + block.shape)
    return lax.all_to_all(many, axes, split_axis=0, concat_axis=0, tiled=False)


def shards(query, cache, new_kv, lengths, hidden_in, out_proj, final_gain, lm_head, tokens, mu):
    nz, nx, ny, nc = (lax.axis_size(a) for a in ("z", "x", "y", "c"))
    z, x, y, c = (lax.axis_index(a) for a in ("z", "x", "y", "c"))
    count = query.shape[0]
    heads, columns = out_proj.shape
    sizes = {"z": nz, "x": nx, "y": ny, "c": nc}

    def from_along_x(block, step):
        return lax.ppermute(block, "x", [(i, (i + step) % nx) for i in range(nx)])

    table = jnp.concatenate([out_proj.T] + [from_along_x(out_proj.T, k) for k in range(1, nx)], axis=0)
    many, *tails = pl.pallas_call(
        functools.partial(attend_kernel, HEADS // KV_HEADS, sizes),
        out_shape=[jax.ShapeDtypeStruct((nz,) + query.shape, bf16)]
        + [jax.ShapeDtypeStruct((TAIL, columns), bf16)] * nx,
        in_specs=[IN_SMEM] + [IN_VMEM] * 4 + [IN_PLACE],
        out_specs=[IN_VMEM] * (nx + 1),
        scratch_shapes=[
            pltpu.VMEM(cache.shape, bf16),
            pltpu.VMEM((count * 8, HEAD_DIM), f32),
            pltpu.VMEM((count * 8, HEAD_DIM), f32),
            pltpu.SemaphoreType.DMA((2, count)),
        ],
        compiler_params=WHOLE,
        name="attend",
    )(lengths, query, new_kv, hidden_in.T, final_gain[None], cache)
    tails = [tails[0]] + [from_along_x(tails[k], k) for k in range(1, nx)]
    gathered = lax.all_to_all(many, "z", split_axis=0, concat_axis=0, tiled=False)
    gathered = gathered.reshape(nz * count, -1)
    partial = lax.dot_general(
        gathered, table, (((1,), (1,)), ((), ())), preferred_element_type=f32
    )
    partial = partial.reshape(nz, count, nx * columns)
    partial = lax.all_to_all(partial, ("c", "y"), split_axis=0, concat_axis=0, tiled=False)

    width = nx * columns
    rows = pl.pallas_call(
        resid_kernel,
        out_shape=jax.ShapeDtypeStruct((nz, count, width + LANES), bf16),
        in_specs=[IN_VMEM] * (nx + 1),
        out_specs=IN_VMEM,
        compiler_params=SMALL,
        name="resid",
    )(partial, *tails)
    rows = lax.all_to_all(rows, "z", split_axis=0, concat_axis=0, tiled=False)
    half = pl.pallas_call(
        norm_kernel,
        out_shape=jax.ShapeDtypeStruct((nx * ny, count, nz * width), bf16),
        in_specs=[IN_VMEM],
        out_specs=IN_VMEM,
        compiler_params=SMALL,
        name="norm",
    )(rows)
    half = lax.all_to_all(half, ("x", "y"), split_axis=0, concat_axis=0, tiled=False)
    other = lax.ppermute(half, "c", [(i, 1 - i) for i in range(2)])
    head = pl.pallas_call(
        fetch_kernel,
        out_shape=jax.ShapeDtypeStruct(lm_head.shape, bf16),
        in_specs=[IN_PLACE] * 2,
        out_specs=IN_VMEM,
        scratch_shapes=[pltpu.SemaphoreType.DMA],
        compiler_params=WIDE,
        name="fetch",
    )(lm_head, half)
    other, head = lax.optimization_barrier((other, head))
    half, other = (
        jnp.swapaxes(h.reshape(nx, ny, count, -1), 0, 1).reshape(nx * ny * count, -1) for h in (half, other)
    )
    first = jnp.where(c == 0, half, other)
    second = jnp.where(c == 0, other, half)
    everyone = jnp.concatenate([first, second], axis=0)

    vocab = lm_head.shape[0]
    requests = everyone.shape[0]
    offset = (((z * nx + x) * ny + y) * nc + c) * vocab
    logits, stats = pl.pallas_call(
        logits_kernel,
        out_shape=[jax.ShapeDtypeStruct((vocab, requests), f32), jax.ShapeDtypeStruct((2, requests), f32)],
        in_specs=[IN_VMEM] * 3,
        out_specs=[IN_VMEM] * 2,
        compiler_params=SMALL,
        name="logits",
    )(head, everyone, (tokens - offset)[None])

    stats = spread(stats, ("x", "y", "c"), nx * ny * nc)
    top = jnp.max(stats[:, 0], axis=0)
    log_mass = top + jnp.log(jnp.sum(jnp.exp(stats[:, 0] - top[None, :]), axis=0))
    picked = jnp.sum(stats[:, 1], axis=0)
    stats = spread(jnp.stack([log_mass, picked]), "z", nz)
    row_shape = jax.ShapeDtypeStruct((1, requests), f32)
    logprobs, surprise, mu_next = pl.pallas_call(
        final_kernel,
        out_shape=[jax.ShapeDtypeStruct((vocab, requests), f32), row_shape, row_shape],
        in_specs=[IN_VMEM] * 3,
        out_specs=[IN_VMEM] * 3,
        compiler_params=SMALL,
        name="final",
    )(logits, stats, mu[None])
    return (logprobs.T, surprise[0], mu_next[0])


def solution(mesh):
    grid = Mesh(np.asarray(mesh.devices).reshape(8, 4, 4, 2), ("z", "x", "y", "c"))
    dp, tensor = ("z", "x"), ("y", "c")
    placed = (
        P(dp, tensor),
        P(dp, None, None, tensor),
        P(dp, None, tensor),
        P(),
        P(None, dp),
        P(tensor, dp),
        P(dp),
        P(dp + tensor, None),
        P(),
        P(),
    )
    return jax.shard_map(
        shards,
        mesh=grid,
        in_specs=placed,
        out_specs=(P(None, dp + tensor), P(), P()),
        check_vma=False,
    )
```

```python
import functools
import math

import jax
import jax.numpy as jnp
import numpy as np
from jax import lax
from jax.experimental import pallas as pl
from jax.experimental.pallas import tpu as pltpu
from jax.sharding import Mesh
from jax.sharding import PartitionSpec as P

D = 5120
HEADS = 40
KV_HEADS = 8
HEAD_DIM = 128

masked_score = -1e30
epsilon = 1e-06
learn_rate = 0.1
target_bits = 5.0

bf16 = jnp.bfloat16
f32 = jnp.float32
LANES = 128

IN_VMEM = pl.BlockSpec(memory_space=pltpu.VMEM)
IN_SMEM = pl.BlockSpec(memory_space=pltpu.SMEM)
IN_PLACE = pl.BlockSpec(memory_space=pl.ANY)
SMALL = pltpu.CompilerParams(vmem_limit_bytes=20 << 20)
WIDE = pltpu.CompilerParams(vmem_limit_bytes=44 << 20)
WHOLE = pltpu.CompilerParams(vmem_limit_bytes=60 << 20)
TAIL = 16
CHUNK = 1280


def three_parts(wide):
    first = wide.astype(bf16).astype(f32)
    rest = wide - first
    second = rest.astype(bf16).astype(f32)
    third = (rest - second).astype(bf16).astype(f32)
    return first, second, third


def tails_of(count, part, x, hidden_ref, gain_ref, tail_refs):
    columns, requests = hidden_ref.shape
    row = lax.broadcasted_iota(jnp.int32, (count, requests), 0)
    lane = lax.broadcasted_iota(jnp.int32, (count, requests), 1)
    parts = three_parts(gain_ref[...])
    below = jnp.concatenate(parts + (jnp.zeros((TAIL - count - 3, columns), f32),), axis=0)
    for step, tail_ref in enumerate(tail_refs):
        target = lax.rem(x + step, len(tail_refs))
        place = (part * len(tail_refs) + target) * count
        chosen = jnp.where(lane == row + place, 1.0, 0.0).astype(bf16)
        hidden = lax.dot_general(
            chosen, hidden_ref[...], (((1,), (1,)), ((), ())), preferred_element_type=f32
        )
        tail_ref[...] = jnp.concatenate([hidden, below], axis=0).astype(bf16)


def attend_kernel(group, sizes, lengths_ref, query_ref, new_ref, hidden_ref, gain_ref, cache_ref, *refs):
    out_ref, tail_refs, (slots_ref, rows_ref, sums_ref, sems) = refs[0], refs[1:-4], refs[-4:]
    count, _, slots, head_dim = cache_ref.shape
    z, x, y, c = (lax.axis_index(a) for a in ("z", "x", "y", "c"))
    scale = head_dim ** (-0.5)
    loads = [
        [
            pltpu.make_async_copy(cache_ref.at[r, kind], slots_ref.at[r, kind], sems.at[kind, r])
            for r in range(count)
        ]
        for kind in range(2)
    ]
    for load in loads[0]:
        load.start()
    tails_of(count, c * sizes["y"] + y, x, hidden_ref, gain_ref, tail_refs)

    query = query_ref[...].astype(f32)
    fresh = new_ref[...].astype(f32)
    rows_ref[...] = jnp.zeros_like(rows_ref)
    for g in range(group):
        rows_ref[pl.ds(g, count, stride=8), :] = query[:, g * head_dim : (g + 1) * head_dim]
    heads = rows_ref[...]
    new_keys = jnp.concatenate([jnp.broadcast_to(fresh[r, 0:1], (8, head_dim)) for r in range(count)], axis=0)
    own_score = jnp.sum(heads * new_keys, axis=1, keepdims=True) * scale
    heads = heads.astype(bf16)
    position = lax.broadcasted_iota(jnp.int32, (8, slots), 1)
    base = (z * sizes["x"] + x) * count
    for load in loads[0]:
        load.wait()
    for load in loads[1]:
        load.start()
    scores = []
    for r in range(count):
        score = lax.dot_general(
            heads[8 * r : 8 * r + 8],
            slots_ref[r, 0],
            (((1,), (1,)), ((), ())),
            preferred_element_type=f32,
        )
        scores.append(jnp.where(position < lengths_ref[base + r], score * scale, masked_score))
    scores = jnp.concatenate(scores, axis=0)
    top = jnp.maximum(jnp.max(scores, axis=1, keepdims=True), own_score)
    weights = jnp.exp(scores - top)
    own_weight = jnp.exp(own_score - top)
    mass = jnp.sum(weights, axis=1, keepdims=True) + own_weight
    parts = three_parts(weights)
    for load in loads[1]:
        load.wait()
    for r in range(count):
        span = slice(8 * r, 8 * r + 8)
        stacked = jnp.concatenate([part[span] for part in parts], axis=0).astype(bf16)
        sums = jnp.dot(stacked, slots_ref[r, 1], preferred_element_type=f32)
        total = sums[:8] + sums[8:16] + sums[16:24] + own_weight[span] * fresh[r, 1:2]
        sums_ref[span] = total / mass[span]
    done = jnp.concatenate([sums_ref[pl.ds(g, count, stride=8), :] for g in range(group)], axis=1).astype(bf16)
    for k in range(out_ref.shape[0]):
        out_ref[k] = done


def resid_kernel(partial_ref, *refs):
    tails, out_ref = refs[:-1], refs[-1]
    count, width = partial_ref.shape[1:]
    columns = width // len(tails)
    total = partial_ref[0]
    for k in range(1, partial_ref.shape[0]):
        total = total + partial_ref[k]
    squares = jnp.zeros((count, 1), f32)
    blocks = []
    for step, tail_ref in enumerate(tails):
        tail = tail_ref[...].astype(f32)
        gain = tail[count : count + 1] + tail[count + 1 : count + 2] + tail[count + 2 : count + 3]
        resid = total[:, step * columns : (step + 1) * columns] + tail[:count]
        resid = resid.astype(bf16).astype(f32)
        squares = squares + jnp.sum(resid * resid, axis=1, keepdims=True)
        blocks.append(resid * gain)
    shift = lax.rem(lax.axis_index("x") + 1, len(tails)) * columns
    ordered = pltpu.roll(jnp.concatenate(blocks[::-1], axis=1), shift, 1)
    lane = lax.broadcasted_iota(jnp.int32, (count, LANES), 1)
    spare = jnp.zeros((count, LANES), f32)
    for k, part in enumerate(three_parts(squares)):
        spare = jnp.where(lane == k, part, spare)
    done = jnp.concatenate([ordered, spare], axis=1).astype(bf16)
    for k in range(out_ref.shape[0]):
        out_ref[k] = done


def norm_kernel(rows_ref, out_ref):
    blocks, count, padded = rows_ref.shape
    width = padded - LANES
    squares = jnp.zeros((count, LANES), f32)
    for k in range(blocks):
        squares = squares + rows_ref[k, :, width:].astype(f32)
    factor = lax.rsqrt(jnp.sum(squares, axis=1, keepdims=True) / D + epsilon)
    for k in range(blocks):
        done = (rows_ref[k, :, :width].astype(f32) * factor).astype(bf16)
        for copy in range(out_ref.shape[0]):
            out_ref[copy, :, k * width : (k + 1) * width] = done


def fetch_kernel(head_hbm, after_ref, head_ref, sem):
    load = pltpu.make_async_copy(head_hbm, head_ref, sem)
    load.start()
    load.wait()


def logits_kernel(head_ref, rows_ref, ids_ref, logits_ref, stats_ref):
    depth = head_ref.shape[1]
    for k in range(depth // CHUNK):
        span = slice(k * CHUNK, (k + 1) * CHUNK)
        product = lax.dot_general(
            head_ref[:, span], rows_ref[:, span], (((1,), (1,)), ((), ())), preferred_element_type=f32
        )
        if k == 0:
            logits_ref[...] = product
        else:
            logits_ref[...] += product
    logits = logits_ref[...]
    top = jnp.max(logits, axis=0, keepdims=True)
    log_mass = top + jnp.log(jnp.sum(jnp.exp(logits - top), axis=0, keepdims=True))
    hits = lax.broadcasted_iota(jnp.int32, logits.shape, 0) == ids_ref[...]
    picked = jnp.sum(jnp.where(hits, logits, 0.0), axis=0, keepdims=True)
    stats_ref[...] = jnp.concatenate([log_mass, picked], axis=0)


def final_kernel(logits_ref, stats_ref, mu_ref, logprobs_ref, surprise_ref, mu_next_ref):
    masses = stats_ref[:, 0]
    top = jnp.max(masses, axis=0, keepdims=True)
    log_mass = top + jnp.log(jnp.sum(jnp.exp(masses - top), axis=0, keepdims=True))
    picked = jnp.sum(stats_ref[:, 1], axis=0, keepdims=True)
    logprobs_ref[...] = logits_ref[...] - log_mass
    surprise = (log_mass - picked) / math.log(2.0)
    surprise_ref[...] = surprise
    mu_next_ref[...] = mu_ref[...] - learn_rate * (surprise - target_bits)


def spread(block, axes, count):
    many = jnp.broadcast_to(block[None], (count,) + block.shape)
    return lax.all_to_all(many, axes, split_axis=0, concat_axis=0, tiled=False)


def shards(query, cache, new_kv, lengths, hidden_in, out_proj, final_gain, lm_head, tokens, mu):
    nz, nx, ny, nc = (lax.axis_size(a) for a in ("z", "x", "y", "c"))
    z, x, y, c = (lax.axis_index(a) for a in ("z", "x", "y", "c"))
    count = query.shape[0]
    heads, columns = out_proj.shape
    sizes = {"z": nz, "x": nx, "y": ny, "c": nc}

    def from_along_x(block, step):
        return lax.ppermute(block, "x", [(i, (i + step) % nx) for i in range(nx)])

    table = jnp.concatenate([out_proj.T] + [from_along_x(out_proj.T, k) for k in range(1, nx)], axis=0)
    many, *tails = pl.pallas_call(
        functools.partial(attend_kernel, HEADS // KV_HEADS, sizes),
        out_shape=[jax.ShapeDtypeStruct((nz,) + query.shape, bf16)]
        + [jax.ShapeDtypeStruct((TAIL, columns), bf16)] * nx,
        in_specs=[IN_SMEM] + [IN_VMEM] * 4 + [IN_PLACE],
        out_specs=[IN_VMEM] * (nx + 1),
        scratch_shapes=[
            pltpu.VMEM(cache.shape, bf16),
            pltpu.VMEM((count * 8, HEAD_DIM), f32),
            pltpu.VMEM((count * 8, HEAD_DIM), f32),
            pltpu.SemaphoreType.DMA((2, count)),
        ],
        compiler_params=WHOLE,
        name="attend",
    )(lengths, query, new_kv, hidden_in.T, final_gain[None], cache)
    tails = [tails[0]] + [from_along_x(tails[k], k) for k in range(1, nx)]
    gathered = lax.all_to_all(many, "z", split_axis=0, concat_axis=0, tiled=False)
    gathered, tails = lax.optimization_barrier((gathered, tails))
    gathered = gathered.reshape(nz * count, -1)
    partial = lax.dot_general(
        gathered, table, (((1,), (1,)), ((), ())), preferred_element_type=f32
    )
    partial = partial.reshape(nz, count, nx * columns)
    partial = lax.all_to_all(partial, ("c", "y"), split_axis=0, concat_axis=0, tiled=False)

    width = nx * columns
    rows = pl.pallas_call(
        resid_kernel,
        out_shape=jax.ShapeDtypeStruct((nz, count, width + LANES), bf16),
        in_specs=[IN_VMEM] * (nx + 1),
        out_specs=IN_VMEM,
        compiler_params=SMALL,
        name="resid",
    )(partial, *tails)
    rows = lax.all_to_all(rows, "z", split_axis=0, concat_axis=0, tiled=False)
    half = pl.pallas_call(
        norm_kernel,
        out_shape=jax.ShapeDtypeStruct((nx * ny, count, nz * width), bf16),
        in_specs=[IN_VMEM],
        out_specs=IN_VMEM,
        compiler_params=SMALL,
        name="norm",
    )(rows)
    half = lax.all_to_all(half, ("y", "x"), split_axis=0, concat_axis=0, tiled=False)
    half = half.reshape(ny * nx * count, -1)
    other = lax.ppermute(half, "c", [(i, 1 - i) for i in range(2)])
    head = pl.pallas_call(
        fetch_kernel,
        out_shape=jax.ShapeDtypeStruct(lm_head.shape, bf16),
        in_specs=[IN_PLACE] * 2,
        out_specs=IN_VMEM,
        scratch_shapes=[pltpu.SemaphoreType.DMA],
        compiler_params=WIDE,
        name="fetch",
    )(lm_head, half)
    other, head = lax.optimization_barrier((other, head))
    first = jnp.where(c == 0, half, other)
    second = jnp.where(c == 0, other, half)
    everyone = jnp.concatenate([first, second], axis=0)

    vocab = lm_head.shape[0]
    requests = everyone.shape[0]
    offset = (((z * nx + x) * ny + y) * nc + c) * vocab
    logits, stats = pl.pallas_call(
        logits_kernel,
        out_shape=[jax.ShapeDtypeStruct((vocab, requests), f32), jax.ShapeDtypeStruct((2, requests), f32)],
        in_specs=[IN_VMEM] * 3,
        out_specs=[IN_VMEM] * 2,
        compiler_params=SMALL,
        name="logits",
    )(head, everyone, (tokens - offset)[None])

    stats = spread(stats, ("x", "y", "c"), nx * ny * nc)
    top = jnp.max(stats[:, 0], axis=0)
    log_mass = top + jnp.log(jnp.sum(jnp.exp(stats[:, 0] - top[None, :]), axis=0))
    picked = jnp.sum(stats[:, 1], axis=0)
    stats = spread(jnp.stack([log_mass, picked]), "z", nz)
    row_shape = jax.ShapeDtypeStruct((1, requests), f32)
    logprobs, surprise, mu_next = pl.pallas_call(
        final_kernel,
        out_shape=[jax.ShapeDtypeStruct((vocab, requests), f32), row_shape, row_shape],
        in_specs=[IN_VMEM] * 3,
        out_specs=[IN_VMEM] * 3,
        compiler_params=SMALL,
        name="final",
    )(logits, stats, mu[None])
    return (logprobs.T, surprise[0], mu_next[0])


def solution(mesh):
    grid = Mesh(np.asarray(mesh.devices).reshape(8, 4, 4, 2), ("z", "x", "y", "c"))
    dp, tensor = ("z", "x"), ("y", "c")
    placed = (
        P(dp, tensor),
        P(dp, None, None, tensor),
        P(dp, None, tensor),
        P(),
        P(None, dp),
        P(tensor, dp),
        P(dp),
        P(dp + tensor, None),
        P(),
        P(),
    )
    return jax.shard_map(
        shards,
        mesh=grid,
        in_specs=placed,
        out_specs=(P(None, dp + tensor), P(), P()),
        check_vma=False,
    )
```

```python
import functools
import math

import jax
import jax.numpy as jnp
import numpy as np
from jax import lax
from jax.experimental import pallas as pl
from jax.experimental.pallas import tpu as pltpu
from jax.sharding import Mesh
from jax.sharding import PartitionSpec as P

D = 5120
HEADS = 40
KV_HEADS = 8
HEAD_DIM = 128

masked_score = -1e30
epsilon = 1e-06
learn_rate = 0.1
target_bits = 5.0

bf16 = jnp.bfloat16
f32 = jnp.float32
LANES = 128

IN_VMEM = pl.BlockSpec(memory_space=pltpu.VMEM)
IN_SMEM = pl.BlockSpec(memory_space=pltpu.SMEM)
IN_PLACE = pl.BlockSpec(memory_space=pl.ANY)
SMALL = pltpu.CompilerParams(vmem_limit_bytes=20 << 20)
WIDE = pltpu.CompilerParams(vmem_limit_bytes=44 << 20)
WHOLE = pltpu.CompilerParams(vmem_limit_bytes=60 << 20)
CHUNK = 1280


def three_parts(wide):
    first = wide.astype(bf16).astype(f32)
    rest = wide - first
    second = rest.astype(bf16).astype(f32)
    third = (rest - second).astype(bf16).astype(f32)
    return first, second, third


def side_by_side(rows):
    return jnp.concatenate([rows[k : k + 8] for k in range(0, rows.shape[0], 8)], axis=1)


def local_terms(part, hidden_ref, gain_ref, terms_ref):
    columns, requests = hidden_ref.shape
    groups = terms_ref.shape[1] // columns
    rows = groups * 8
    row = lax.broadcasted_iota(jnp.int32, (rows, requests), 0)
    lane = lax.broadcasted_iota(jnp.int32, (rows, requests), 1)
    chosen = jnp.where(lane == row + part * rows, 1.0, 0.0).astype(bf16)
    hidden = lax.dot_general(
        chosen, hidden_ref[...], (((1,), (1,)), ((), ())), preferred_element_type=f32
    )
    terms_ref[:8] = side_by_side(hidden)
    gain = jnp.broadcast_to(gain_ref[...], (8, columns))
    terms_ref[8:] = jnp.concatenate([gain] * groups, axis=1)


def attend_kernel(group, sizes, lengths_ref, query_ref, new_ref, hidden_ref, gain_ref, cache_ref, out_ref, terms_ref, slots_ref, rows_ref, sums_ref, sems):
    count, _, slots, head_dim = cache_ref.shape
    z, x, y, c = (lax.axis_index(a) for a in ("z", "x", "y", "c"))
    scale = head_dim ** (-0.5)
    loads = [
        [
            pltpu.make_async_copy(cache_ref.at[r, kind], slots_ref.at[r, kind], sems.at[kind, r])
            for r in range(count)
        ]
        for kind in range(2)
    ]
    for load in loads[0] + loads[1]:
        load.start()
    local_terms(c * sizes["y"] + y, hidden_ref, gain_ref, terms_ref)

    query = query_ref[...].astype(f32)
    fresh = new_ref[...].astype(f32)
    rows_ref[...] = jnp.zeros_like(rows_ref)
    for g in range(group):
        rows_ref[pl.ds(g, count, stride=8), :] = query[:, g * head_dim : (g + 1) * head_dim]
    heads = rows_ref[...]
    new_keys = jnp.concatenate([jnp.broadcast_to(fresh[r, 0:1], (8, head_dim)) for r in range(count)], axis=0)
    own_score = jnp.sum(heads * new_keys, axis=1, keepdims=True) * scale
    heads = heads.astype(bf16)
    position = lax.broadcasted_iota(jnp.int32, (8, slots), 1)
    base = (z * sizes["x"] + x) * count
    for load in loads[0]:
        load.wait()
    scores = []
    for r in range(count):
        score = lax.dot_general(
            heads[8 * r : 8 * r + 8],
            slots_ref[r, 0],
            (((1,), (1,)), ((), ())),
            preferred_element_type=f32,
        )
        scores.append(jnp.where(position < lengths_ref[base + r], score * scale, masked_score))
    scores = jnp.concatenate(scores, axis=0)
    top = jnp.maximum(jnp.max(scores, axis=1, keepdims=True), own_score)
    weights = jnp.exp(scores - top)
    own_weight = jnp.exp(own_score - top)
    mass = jnp.sum(weights, axis=1, keepdims=True) + own_weight
    parts = three_parts(weights)
    for load in loads[1]:
        load.wait()
    for r in range(count):
        span = slice(8 * r, 8 * r + 8)
        stacked = jnp.concatenate([part[span] for part in parts], axis=0).astype(bf16)
        sums = jnp.dot(stacked, slots_ref[r, 1], preferred_element_type=f32)
        total = sums[:8] + sums[8:16] + sums[16:24] + own_weight[span] * fresh[r, 1:2]
        sums_ref[span] = total / mass[span]
    done = jnp.concatenate([sums_ref[pl.ds(g, count, stride=8), :] for g in range(group)], axis=1).astype(bf16)
    for k in range(out_ref.shape[0]):
        out_ref[k] = done


def project_kernel(rows_ref, table_ref, out_ref):
    product = lax.dot_general(
        rows_ref[...], table_ref[...], (((1,), (1,)), ((), ())), preferred_element_type=f32
    )
    size = product.shape[0] // out_ref.shape[0]
    for k in range(out_ref.shape[0]):
        out_ref[k] = side_by_side(product[k * size : (k + 1) * size])


def resid_kernel(columns, partial_ref, terms_ref, out_ref):
    count, width = partial_ref.shape[1:]
    total = partial_ref[0]
    for k in range(1, partial_ref.shape[0]):
        total = total + partial_ref[k]
    resid = (total + terms_ref[:count]).astype(bf16).astype(f32)
    lane = lax.broadcasted_iota(jnp.int32, (count, LANES), 1)
    spare = jnp.zeros((count, LANES), f32)
    for g in range(width // columns):
        piece = resid[:, g * columns : (g + 1) * columns]
        for k, part in enumerate(three_parts(jnp.sum(piece * piece, axis=1, keepdims=True))):
            spare = jnp.where(lane == 3 * g + k, part, spare)
    done = jnp.concatenate([resid * terms_ref[count:], spare], axis=1).astype(bf16)
    for k in range(out_ref.shape[0]):
        out_ref[k] = done


def norm_kernel(columns, rows_ref, out_ref):
    sources, count, padded = rows_ref.shape
    width = padded - LANES
    squares = jnp.zeros((count, LANES), f32)
    for k in range(sources):
        squares = squares + rows_ref[k, :, width:].astype(f32)
    lane = lax.broadcasted_iota(jnp.int32, (count, LANES), 1)
    factors = []
    for g in range(width // columns):
        mine = jnp.where((lane >= 3 * g) & (lane < 3 * g + 3), squares, 0.0)
        factors.append(lax.rsqrt(jnp.sum(mine, axis=1, keepdims=True) / D + epsilon))
    for k in range(0, sources, 4):
        blocks = [rows_ref[k + i, :, :width].astype(f32) for i in range(4)]
        rows = [
            jnp.concatenate([b[:, g * columns : (g + 1) * columns] for b in blocks], axis=1) * factors[g]
            for g in range(width // columns)
        ]
        out_ref[:, k * columns : (k + 4) * columns] = jnp.concatenate(rows, axis=0).astype(bf16)


def fetch_kernel(head_hbm, after_ref, head_ref, sem):
    load = pltpu.make_async_copy(head_hbm, head_ref, sem)
    load.start()
    load.wait()


def logits_kernel(head_ref, ids_ref, *refs):
    blocks, (logits_ref, stats_ref, rows_ref) = refs[:-3], refs[-3:]
    y, c = lax.axis_index("y"), lax.axis_index("c")
    depth = head_ref.shape[1]
    number = len(blocks) // 2
    size = blocks[0].shape[0]
    for k, block in enumerate(blocks):
        core = c if k < number else 1 - c
        place = core * number + lax.rem(y + k % number, number)
        rows_ref[pl.ds(pl.multiple_of(place * size, size), size), :] = block[...]
    for k in range(depth // CHUNK):
        span = slice(k * CHUNK, (k + 1) * CHUNK)
        product = lax.dot_general(
            head_ref[:, span], rows_ref[:, span], (((1,), (1,)), ((), ())), preferred_element_type=f32
        )
        if k == 0:
            logits_ref[...] = product
        else:
            logits_ref[...] += product
    logits = logits_ref[...]
    top = jnp.max(logits, axis=0, keepdims=True)
    log_mass = top + jnp.log(jnp.sum(jnp.exp(logits - top), axis=0, keepdims=True))
    hits = lax.broadcasted_iota(jnp.int32, logits.shape, 0) == ids_ref[...]
    picked = jnp.sum(jnp.where(hits, logits, 0.0), axis=0, keepdims=True)
    stats_ref[...] = jnp.concatenate([log_mass, picked], axis=0)


def final_kernel(logits_ref, stats_ref, mu_ref, logprobs_ref, surprise_ref, mu_next_ref):
    masses = stats_ref[:, 0]
    top = jnp.max(masses, axis=0, keepdims=True)
    log_mass = top + jnp.log(jnp.sum(jnp.exp(masses - top), axis=0, keepdims=True))
    picked = jnp.sum(stats_ref[:, 1], axis=0, keepdims=True)
    logprobs_ref[...] = logits_ref[...] - log_mass
    surprise = (log_mass - picked) / math.log(2.0)
    surprise_ref[...] = surprise
    mu_next_ref[...] = mu_ref[...] - learn_rate * (surprise - target_bits)


def spread(block, axes, count):
    many = jnp.broadcast_to(block[None], (count,) + block.shape)
    return lax.all_to_all(many, axes, split_axis=0, concat_axis=0, tiled=False)


def shards(query, cache, new_kv, lengths, hidden_in, out_proj, final_gain, lm_head, tokens, mu):
    nz, nx, ny, nc = (lax.axis_size(a) for a in ("z", "x", "y", "c"))
    z, x, y, c = (lax.axis_index(a) for a in ("z", "x", "y", "c"))
    count = query.shape[0]
    heads, columns = out_proj.shape
    requests = hidden_in.shape[0]
    share = requests // (ny * nc)
    width = share // 8 * columns
    sizes = {"z": nz, "x": nx, "y": ny, "c": nc}

    many, terms = pl.pallas_call(
        functools.partial(attend_kernel, HEADS // KV_HEADS, sizes),
        out_shape=[
            jax.ShapeDtypeStruct((nz * nx,) + query.shape, bf16),
            jax.ShapeDtypeStruct((16, width), f32),
        ],
        in_specs=[IN_SMEM] + [IN_VMEM] * 4 + [IN_PLACE],
        out_specs=[IN_VMEM] * 2,
        scratch_shapes=[
            pltpu.VMEM(cache.shape, bf16),
            pltpu.VMEM((count * 8, HEAD_DIM), f32),
            pltpu.VMEM((count * 8, HEAD_DIM), f32),
            pltpu.SemaphoreType.DMA((2, count)),
        ],
        compiler_params=WHOLE,
        name="attend",
    )(lengths, query, new_kv, hidden_in.T, final_gain[None], cache)
    gathered = lax.all_to_all(many, ("z", "x"), split_axis=0, concat_axis=0, tiled=False)
    partial = pl.pallas_call(
        project_kernel,
        out_shape=jax.ShapeDtypeStruct((ny * nc, 8, width), f32),
        in_specs=[IN_VMEM] * 2,
        out_specs=IN_VMEM,
        compiler_params=SMALL,
        name="project",
    )(gathered.reshape(requests, heads), out_proj.T)
    partial = lax.all_to_all(partial, ("c", "y"), split_axis=0, concat_axis=0, tiled=False)
    rows = pl.pallas_call(
        functools.partial(resid_kernel, columns),
        out_shape=jax.ShapeDtypeStruct((nz * nx, 8, width + LANES), bf16),
        in_specs=[IN_VMEM] * 2,
        out_specs=IN_VMEM,
        compiler_params=SMALL,
        name="resid",
    )(partial, terms)
    rows = lax.all_to_all(rows, ("z", "x"), split_axis=0, concat_axis=0, tiled=False)
    own = pl.pallas_call(
        functools.partial(norm_kernel, columns),
        out_shape=jax.ShapeDtypeStruct((share, nz * nx * columns), bf16),
        in_specs=[IN_VMEM],
        out_specs=IN_VMEM,
        compiler_params=SMALL,
        name="norm",
    )(rows)

    def along_y(block, step):
        return lax.ppermute(block, "y", [(i, (i + step) % ny) for i in range(ny)])

    def to_other_core(block):
        return lax.ppermute(block, "c", [(i, 1 - i) for i in range(nc)])

    before, after = along_y(own, 1), along_y(own, -1)
    opposite = jnp.concatenate(
        [along_y(after[: share // 2], -1), along_y(before[share // 2 :], 1)], axis=0
    )
    mine = [own, after, opposite, before]
    other = jnp.split(to_other_core(jnp.concatenate([own, after, before], axis=0)), 3, axis=0)
    last = to_other_core(opposite)
    theirs = [other[0], other[1], last, other[2]]
    head = pl.pallas_call(
        fetch_kernel,
        out_shape=jax.ShapeDtypeStruct(lm_head.shape, bf16),
        in_specs=[IN_PLACE] * 2,
        out_specs=IN_VMEM,
        scratch_shapes=[pltpu.SemaphoreType.DMA],
        compiler_params=WIDE,
        name="fetch",
    )(lm_head, before)
    theirs, head = lax.optimization_barrier((theirs, head))

    vocab = lm_head.shape[0]
    offset = (((z * nx + x) * ny + y) * nc + c) * vocab
    logits, stats = pl.pallas_call(
        logits_kernel,
        out_shape=[jax.ShapeDtypeStruct((vocab, requests), f32), jax.ShapeDtypeStruct((2, requests), f32)],
        in_specs=[IN_VMEM] * (2 + 2 * ny),
        out_specs=[IN_VMEM] * 2,
        scratch_shapes=[pltpu.VMEM((requests, lm_head.shape[1]), bf16)],
        compiler_params=SMALL,
        name="logits",
    )(head, (tokens - offset)[None], *mine, *theirs)

    stats = spread(stats, ("x", "y", "c"), nx * ny * nc)
    top = jnp.max(stats[:, 0], axis=0)
    log_mass = top + jnp.log(jnp.sum(jnp.exp(stats[:, 0] - top[None, :]), axis=0))
    picked = jnp.sum(stats[:, 1], axis=0)
    stats = spread(jnp.stack([log_mass, picked]), "z", nz)
    row_shape = jax.ShapeDtypeStruct((1, requests), f32)
    logprobs, surprise, mu_next = pl.pallas_call(
        final_kernel,
        out_shape=[jax.ShapeDtypeStruct((vocab, requests), f32), row_shape, row_shape],
        in_specs=[IN_VMEM] * 3,
        out_specs=[IN_VMEM] * 3,
        compiler_params=SMALL,
        name="final",
    )(logits, stats, mu[None])
    return (logprobs.T, surprise[0], mu_next[0])


def solution(mesh):
    grid = Mesh(np.asarray(mesh.devices).reshape(8, 4, 4, 2), ("z", "x", "y", "c"))
    dp, tensor = ("z", "x"), ("y", "c")
    placed = (
        P(dp, tensor),
        P(dp, None, None, tensor),
        P(dp, None, tensor),
        P(),
        P(None, dp),
        P(tensor, dp),
        P(dp),
        P(dp + tensor, None),
        P(),
        P(),
    )
    return jax.shard_map(
        shards,
        mesh=grid,
        in_specs=placed,
        out_specs=(P(None, dp + tensor), P(), P()),
        check_vma=False,
    )
```

```python
import functools
import math

import jax
import jax.numpy as jnp
import numpy as np
from jax import lax
from jax.experimental import pallas as pl
from jax.experimental.pallas import tpu as pltpu
from jax.sharding import Mesh
from jax.sharding import PartitionSpec as P

D = 5120
HEADS = 40
KV_HEADS = 8
HEAD_DIM = 128

masked_score = -1e30
epsilon = 1e-06
learn_rate = 0.1
target_bits = 5.0

bf16 = jnp.bfloat16
f32 = jnp.float32
LANES = 128

IN_VMEM = pl.BlockSpec(memory_space=pltpu.VMEM)
IN_SMEM = pl.BlockSpec(memory_space=pltpu.SMEM)
IN_PLACE = pl.BlockSpec(memory_space=pl.ANY)
SMALL = pltpu.CompilerParams(vmem_limit_bytes=20 << 20)
WIDE = pltpu.CompilerParams(vmem_limit_bytes=44 << 20)
WHOLE = pltpu.CompilerParams(vmem_limit_bytes=60 << 20)
TAIL = 16
CHUNK = 1280


def three_parts(wide):
    first = wide.astype(bf16).astype(f32)
    rest = wide - first
    second = rest.astype(bf16).astype(f32)
    third = (rest - second).astype(bf16).astype(f32)
    return first, second, third


def tails_of(count, part, x, hidden_ref, gain_ref, tail_refs):
    columns, requests = hidden_ref.shape
    row = lax.broadcasted_iota(jnp.int32, (count, requests), 0)
    lane = lax.broadcasted_iota(jnp.int32, (count, requests), 1)
    parts = three_parts(gain_ref[...])
    below = jnp.concatenate(parts + (jnp.zeros((TAIL - count - 3, columns), f32),), axis=0)
    for step, tail_ref in enumerate(tail_refs):
        target = lax.rem(x + step, len(tail_refs))
        place = (part * len(tail_refs) + target) * count
        chosen = jnp.where(lane == row + place, 1.0, 0.0).astype(bf16)
        hidden = lax.dot_general(
            chosen, hidden_ref[...], (((1,), (1,)), ((), ())), preferred_element_type=f32
        )
        tail_ref[...] = jnp.concatenate([hidden, below], axis=0).astype(bf16)


def attend_kernel(group, sizes, lengths_ref, query_ref, new_ref, hidden_ref, gain_ref, cache_ref, *refs):
    out_ref, tail_refs, (slots_ref, rows_ref, sums_ref, sems) = refs[0], refs[1:-4], refs[-4:]
    count, _, slots, head_dim = cache_ref.shape
    z, x, y, c = (lax.axis_index(a) for a in ("z", "x", "y", "c"))
    scale = head_dim ** (-0.5)
    loads = [
        [
            pltpu.make_async_copy(cache_ref.at[r, kind], slots_ref.at[r, kind], sems.at[kind, r])
            for r in range(count)
        ]
        for kind in range(2)
    ]
    for load in loads[0] + loads[1]:
        load.start()
    tails_of(count, c * sizes["y"] + y, x, hidden_ref, gain_ref, tail_refs)

    query = query_ref[...].astype(f32)
    fresh = new_ref[...].astype(f32)
    rows_ref[...] = jnp.zeros_like(rows_ref)
    for g in range(group):
        rows_ref[pl.ds(g, count, stride=8), :] = query[:, g * head_dim : (g + 1) * head_dim]
    heads = rows_ref[...]
    new_keys = jnp.concatenate([jnp.broadcast_to(fresh[r, 0:1], (8, head_dim)) for r in range(count)], axis=0)
    own_score = jnp.sum(heads * new_keys, axis=1, keepdims=True) * scale
    heads = heads.astype(bf16)
    position = lax.broadcasted_iota(jnp.int32, (8, slots), 1)
    base = (z * sizes["x"] + x) * count
    for load in loads[0]:
        load.wait()
    scores = []
    for r in range(count):
        score = lax.dot_general(
            heads[8 * r : 8 * r + 8],
            slots_ref[r, 0],
            (((1,), (1,)), ((), ())),
            preferred_element_type=f32,
        )
        scores.append(jnp.where(position < lengths_ref[base + r], score * scale, masked_score))
    scores = jnp.concatenate(scores, axis=0)
    top = jnp.maximum(jnp.max(scores, axis=1, keepdims=True), own_score)
    weights = jnp.exp(scores - top)
    own_weight = jnp.exp(own_score - top)
    mass = jnp.sum(weights, axis=1, keepdims=True) + own_weight
    parts = three_parts(weights)
    for load in loads[1]:
        load.wait()
    for r in range(count):
        span = slice(8 * r, 8 * r + 8)
        stacked = jnp.concatenate([part[span] for part in parts], axis=0).astype(bf16)
        sums = jnp.dot(stacked, slots_ref[r, 1], preferred_element_type=f32)
        total = sums[:8] + sums[8:16] + sums[16:24] + own_weight[span] * fresh[r, 1:2]
        sums_ref[span] = total / mass[span]
    done = jnp.concatenate([sums_ref[pl.ds(g, count, stride=8), :] for g in range(group)], axis=1).astype(bf16)
    for k in range(out_ref.shape[0]):
        out_ref[k] = done


def resid_kernel(partial_ref, *refs):
    tails, out_ref = refs[:-1], refs[-1]
    count, width = partial_ref.shape[1:]
    columns = width // len(tails)
    total = partial_ref[0]
    for k in range(1, partial_ref.shape[0]):
        total = total + partial_ref[k]
    squares = jnp.zeros((count, 1), f32)
    blocks = []
    for step, tail_ref in enumerate(tails):
        tail = tail_ref[...].astype(f32)
        gain = tail[count : count + 1] + tail[count + 1 : count + 2] + tail[count + 2 : count + 3]
        resid = total[:, step * columns : (step + 1) * columns] + tail[:count]
        resid = resid.astype(bf16).astype(f32)
        squares = squares + jnp.sum(resid * resid, axis=1, keepdims=True)
        blocks.append(resid * gain)
    shift = lax.rem(lax.axis_index("x") + 1, len(tails)) * columns
    ordered = pltpu.roll(jnp.concatenate(blocks[::-1], axis=1), shift, 1)
    lane = lax.broadcasted_iota(jnp.int32, (count, LANES), 1)
    spare = jnp.zeros((count, LANES), f32)
    for k, part in enumerate(three_parts(squares)):
        spare = jnp.where(lane == k, part, spare)
    done = jnp.concatenate([ordered, spare], axis=1).astype(bf16)
    for k in range(out_ref.shape[0]):
        out_ref[k] = done


def norm_kernel(rows_ref, out_ref):
    blocks, count, padded = rows_ref.shape
    width = padded - LANES
    squares = jnp.zeros((count, LANES), f32)
    for k in range(blocks):
        squares = squares + rows_ref[k, :, width:].astype(f32)
    factor = lax.rsqrt(jnp.sum(squares, axis=1, keepdims=True) / D + epsilon)
    for k in range(blocks):
        out_ref[:, k * width : (k + 1) * width] = (rows_ref[k, :, :width].astype(f32) * factor).astype(bf16)


def order_kernel(*refs):
    blocks, out_ref = [ref[...].astype(f32) for ref in refs[:-1]], refs[-1]
    x = lax.axis_index("x")
    number = len(blocks)
    ordered = []
    for k in range(number):
        ahead = lax.rem(k + number - x, number)
        piece = blocks[0]
        for step in range(1, number):
            piece = jnp.where(ahead == step, blocks[step], piece)
        ordered.append(piece)
    out_ref[...] = jnp.concatenate(ordered, axis=0).astype(bf16)


def fetch_kernel(head_hbm, after_ref, head_ref, sem):
    load = pltpu.make_async_copy(head_hbm, head_ref, sem)
    load.start()
    load.wait()


def logits_kernel(head_ref, ids_ref, *refs):
    blocks, (logits_ref, stats_ref, rows_ref) = refs[:-3], refs[-3:]
    y, c = lax.axis_index("y"), lax.axis_index("c")
    depth = head_ref.shape[1]
    number = len(blocks) // 2
    size = blocks[0].shape[0]
    for k, block in enumerate(blocks):
        core = c if k < number else 1 - c
        place = core * number + lax.rem(y + k % number, number)
        rows_ref[pl.ds(pl.multiple_of(place * size, size), size), :] = block[...]
    for k in range(depth // CHUNK):
        span = slice(k * CHUNK, (k + 1) * CHUNK)
        product = lax.dot_general(
            head_ref[:, span], rows_ref[:, span], (((1,), (1,)), ((), ())), preferred_element_type=f32
        )
        if k == 0:
            logits_ref[...] = product
        else:
            logits_ref[...] += product
    logits = logits_ref[...]
    top = jnp.max(logits, axis=0, keepdims=True)
    log_mass = top + jnp.log(jnp.sum(jnp.exp(logits - top), axis=0, keepdims=True))
    hits = lax.broadcasted_iota(jnp.int32, logits.shape, 0) == ids_ref[...]
    picked = jnp.sum(jnp.where(hits, logits, 0.0), axis=0, keepdims=True)
    stats_ref[...] = jnp.concatenate([log_mass, picked], axis=0)


def final_kernel(logits_ref, stats_ref, mu_ref, logprobs_ref, surprise_ref, mu_next_ref):
    masses = stats_ref[:, 0]
    top = jnp.max(masses, axis=0, keepdims=True)
    log_mass = top + jnp.log(jnp.sum(jnp.exp(masses - top), axis=0, keepdims=True))
    picked = jnp.sum(stats_ref[:, 1], axis=0, keepdims=True)
    logprobs_ref[...] = logits_ref[...] - log_mass
    surprise = (log_mass - picked) / math.log(2.0)
    surprise_ref[...] = surprise
    mu_next_ref[...] = mu_ref[...] - learn_rate * (surprise - target_bits)


def spread(block, axes, count):
    many = jnp.broadcast_to(block[None], (count,) + block.shape)
    return lax.all_to_all(many, axes, split_axis=0, concat_axis=0, tiled=False)


def shards(query, cache, new_kv, lengths, hidden_in, out_proj, final_gain, lm_head, tokens, mu):
    nz, nx, ny, nc = (lax.axis_size(a) for a in ("z", "x", "y", "c"))
    z, x, y, c = (lax.axis_index(a) for a in ("z", "x", "y", "c"))
    count = query.shape[0]
    heads, columns = out_proj.shape
    sizes = {"z": nz, "x": nx, "y": ny, "c": nc}

    def from_along_x(block, step):
        return lax.ppermute(block, "x", [(i, (i + step) % nx) for i in range(nx)])

    table = jnp.concatenate([out_proj.T] + [from_along_x(out_proj.T, k) for k in range(1, nx)], axis=0)
    many, *tails = pl.pallas_call(
        functools.partial(attend_kernel, HEADS // KV_HEADS, sizes),
        out_shape=[jax.ShapeDtypeStruct((nz,) + query.shape, bf16)]
        + [jax.ShapeDtypeStruct((TAIL, columns), bf16)] * nx,
        in_specs=[IN_SMEM] + [IN_VMEM] * 4 + [IN_PLACE],
        out_specs=[IN_VMEM] * (nx + 1),
        scratch_shapes=[
            pltpu.VMEM(cache.shape, bf16),
            pltpu.VMEM((count * 8, HEAD_DIM), f32),
            pltpu.VMEM((count * 8, HEAD_DIM), f32),
            pltpu.SemaphoreType.DMA((2, count)),
        ],
        compiler_params=WHOLE,
        name="attend",
    )(lengths, query, new_kv, hidden_in.T, final_gain[None], cache)
    tails = [tails[0]] + [from_along_x(tails[k], k) for k in range(1, nx)]
    gathered = lax.all_to_all(many, "z", split_axis=0, concat_axis=0, tiled=False)
    gathered = gathered.reshape(nz * count, -1)
    partial = lax.dot_general(
        gathered, table, (((1,), (1,)), ((), ())), preferred_element_type=f32
    )
    partial = partial.reshape(nz, count, nx * columns)
    partial = lax.all_to_all(partial, ("c", "y"), split_axis=0, concat_axis=0, tiled=False)

    width = nx * columns
    rows = pl.pallas_call(
        resid_kernel,
        out_shape=jax.ShapeDtypeStruct((nz, count, width + LANES), bf16),
        in_specs=[IN_VMEM] * (nx + 1),
        out_specs=IN_VMEM,
        compiler_params=SMALL,
        name="resid",
    )(partial, *tails)
    rows = lax.all_to_all(rows, "z", split_axis=0, concat_axis=0, tiled=False)
    normed = pl.pallas_call(
        norm_kernel,
        out_shape=jax.ShapeDtypeStruct((count, nz * width), bf16),
        in_specs=[IN_VMEM],
        out_specs=IN_VMEM,
        compiler_params=SMALL,
        name="norm",
    )(rows)
    share = nx * count
    own = pl.pallas_call(
        order_kernel,
        out_shape=jax.ShapeDtypeStruct((share, nz * width), bf16),
        in_specs=[IN_VMEM] * nx,
        out_specs=IN_VMEM,
        compiler_params=SMALL,
        name="order",
    )(normed, *(from_along_x(normed, nx - k) for k in range(1, nx)))

    def along_y(block, step):
        return lax.ppermute(block, "y", [(i, (i + step) % ny) for i in range(ny)])

    def to_other_core(block):
        return lax.ppermute(block, "c", [(i, 1 - i) for i in range(nc)])

    before, after = along_y(own, 1), along_y(own, -1)
    head = pl.pallas_call(
        fetch_kernel,
        out_shape=jax.ShapeDtypeStruct(lm_head.shape, bf16),
        in_specs=[IN_PLACE] * 2,
        out_specs=IN_VMEM,
        scratch_shapes=[pltpu.SemaphoreType.DMA],
        compiler_params=WIDE,
        name="fetch",
    )(lm_head, own)
    before, after, head = lax.optimization_barrier((before, after, head))
    opposite = jnp.concatenate(
        [along_y(after[: share // 2], -1), along_y(before[share // 2 :], 1)], axis=0
    )
    mine = [own, after, opposite, before]
    other = jnp.split(to_other_core(jnp.concatenate([own, after, before], axis=0)), 3, axis=0)
    last = to_other_core(opposite)
    theirs = [other[0], other[1], last, other[2]]

    vocab = lm_head.shape[0]
    requests = hidden_in.shape[0]
    offset = (((z * nx + x) * ny + y) * nc + c) * vocab
    logits, stats = pl.pallas_call(
        logits_kernel,
        out_shape=[jax.ShapeDtypeStruct((vocab, requests), f32), jax.ShapeDtypeStruct((2, requests), f32)],
        in_specs=[IN_VMEM] * (2 + 2 * ny),
        out_specs=[IN_VMEM] * 2,
        scratch_shapes=[pltpu.VMEM((requests, lm_head.shape[1]), bf16)],
        compiler_params=SMALL,
        name="logits",
    )(head, (tokens - offset)[None], *mine, *theirs)

    stats = spread(stats, ("x", "y", "c"), nx * ny * nc)
    top = jnp.max(stats[:, 0], axis=0)
    log_mass = top + jnp.log(jnp.sum(jnp.exp(stats[:, 0] - top[None, :]), axis=0))
    picked = jnp.sum(stats[:, 1], axis=0)
    stats = spread(jnp.stack([log_mass, picked]), "z", nz)
    row_shape = jax.ShapeDtypeStruct((1, requests), f32)
    logprobs, surprise, mu_next = pl.pallas_call(
        final_kernel,
        out_shape=[jax.ShapeDtypeStruct((vocab, requests), f32), row_shape, row_shape],
        in_specs=[IN_VMEM] * 3,
        out_specs=[IN_VMEM] * 3,
        compiler_params=SMALL,
        name="final",
    )(logits, stats, mu[None])
    return (logprobs.T, surprise[0], mu_next[0])


def solution(mesh):
    grid = Mesh(np.asarray(mesh.devices).reshape(8, 4, 4, 2), ("z", "x", "y", "c"))
    dp, tensor = ("z", "x"), ("y", "c")
    placed = (
        P(dp, tensor),
        P(dp, None, None, tensor),
        P(dp, None, tensor),
        P(),
        P(None, dp),
        P(tensor, dp),
        P(dp),
        P(dp + tensor, None),
        P(),
        P(),
    )
    return jax.shard_map(
        shards,
        mesh=grid,
        in_specs=placed,
        out_specs=(P(None, dp + tensor), P(), P()),
        check_vma=False,
    )
```

```python
import functools
import math

import jax
import jax.numpy as jnp
import numpy as np
from jax import lax
from jax.experimental import pallas as pl
from jax.experimental.pallas import tpu as pltpu
from jax.sharding import Mesh
from jax.sharding import PartitionSpec as P

D = 5120
HEADS = 40
KV_HEADS = 8
HEAD_DIM = 128

masked_score = -1e30
epsilon = 1e-06
learn_rate = 0.1
target_bits = 5.0

bf16 = jnp.bfloat16
f32 = jnp.float32
LANES = 128

IN_VMEM = pl.BlockSpec(memory_space=pltpu.VMEM)
IN_SMEM = pl.BlockSpec(memory_space=pltpu.SMEM)
IN_PLACE = pl.BlockSpec(memory_space=pl.ANY)
SMALL = pltpu.CompilerParams(vmem_limit_bytes=20 << 20)
WIDE = pltpu.CompilerParams(vmem_limit_bytes=44 << 20)
WHOLE = pltpu.CompilerParams(vmem_limit_bytes=60 << 20)
TAIL = 16
CHUNK = 1280


def three_parts(wide):
    first = wide.astype(bf16).astype(f32)
    rest = wide - first
    second = rest.astype(bf16).astype(f32)
    third = (rest - second).astype(bf16).astype(f32)
    return first, second, third


def side_by_side(rows):
    return jnp.concatenate([rows[k : k + 8] for k in range(0, rows.shape[0], 8)], axis=1)


def pack_kernel(sizes, table_hbm, hidden_hbm, gain_hbm, pack_hbm, hidden_ref, gain_ref, tail_ref, sems):
    columns, heads = table_hbm.shape
    table = pltpu.make_async_copy(table_hbm, pack_hbm.at[pl.ds(0, columns)], sems.at[0])
    hidden = pltpu.make_async_copy(hidden_hbm, hidden_ref, sems.at[1])
    gain = pltpu.make_async_copy(gain_hbm, gain_ref, sems.at[2])
    hidden.start()
    gain.start()
    table.start()
    rows, requests = heads // columns * 8, hidden_ref.shape[1]
    part = lax.axis_index("c") * sizes["y"] + lax.axis_index("y")
    row = lax.broadcasted_iota(jnp.int32, (rows, requests), 0)
    lane = lax.broadcasted_iota(jnp.int32, (rows, requests), 1)
    chosen = jnp.where(lane == row + part * rows, 1.0, 0.0).astype(bf16)
    hidden.wait()
    gain.wait()
    picked = lax.dot_general(
        chosen, hidden_ref[...], (((1,), (1,)), ((), ())), preferred_element_type=f32
    )
    below = jnp.concatenate(three_parts(gain_ref[...]) + (jnp.zeros((5, columns), f32),), axis=0)
    below = jnp.concatenate([below, jnp.zeros((8, heads - columns), f32)], axis=1)
    tail_ref[...] = jnp.concatenate([side_by_side(picked), below], axis=0).astype(bf16)
    tail = pltpu.make_async_copy(tail_ref, pack_hbm.at[pl.ds(columns, TAIL)], sems.at[3])
    tail.start()
    table.wait()
    tail.wait()


def attend_kernel(group, sizes, lengths_ref, query_ref, new_ref, cache_ref, out_ref, slots_ref, rows_ref, sums_ref, sems):
    count, _, slots, head_dim = cache_ref.shape
    z, x = lax.axis_index("z"), lax.axis_index("x")
    scale = head_dim ** (-0.5)
    portions = [range(k, k + count // 2) for k in (0, count // 2)]
    loads = [
        [
            pltpu.make_async_copy(cache_ref.at[r, kind], slots_ref.at[r, kind], sems.at[kind, r])
            for r in portion
        ]
        for portion in portions
        for kind in range(2)
    ]
    for load in sum(loads, []):
        load.start()

    query = query_ref[...].astype(f32)
    fresh = new_ref[...].astype(f32)
    rows_ref[...] = jnp.zeros_like(rows_ref)
    for g in range(group):
        rows_ref[pl.ds(g, count, stride=8), :] = query[:, g * head_dim : (g + 1) * head_dim]
    heads = rows_ref[...]
    new_keys = jnp.concatenate([jnp.broadcast_to(fresh[r, 0:1], (8, head_dim)) for r in range(count)], axis=0)
    own_scores = jnp.sum(heads * new_keys, axis=1, keepdims=True) * scale
    heads = heads.astype(bf16)
    position = lax.broadcasted_iota(jnp.int32, (8, slots), 1)
    base = (z * sizes["x"] + x) * count
    for portion, key_loads, value_loads in zip(portions, loads[::2], loads[1::2]):
        for load in key_loads:
            load.wait()
        scores = []
        for r in portion:
            score = lax.dot_general(
                heads[8 * r : 8 * r + 8],
                slots_ref[r, 0],
                (((1,), (1,)), ((), ())),
                preferred_element_type=f32,
            )
            scores.append(jnp.where(position < lengths_ref[base + r], score * scale, masked_score))
        scores = jnp.concatenate(scores, axis=0)
        own_score = own_scores[8 * portion[0] : 8 * portion[0] + scores.shape[0]]
        top = jnp.maximum(jnp.max(scores, axis=1, keepdims=True), own_score)
        weights = jnp.exp(scores - top)
        own_weight = jnp.exp(own_score - top)
        mass = jnp.sum(weights, axis=1, keepdims=True) + own_weight
        coarse = weights.astype(bf16)
        fine = (weights - coarse.astype(f32)).astype(bf16)
        for load in value_loads:
            load.wait()
        for k, r in enumerate(portion):
            span = slice(8 * k, 8 * k + 8)
            stacked = jnp.concatenate([coarse[span].astype(f32), fine[span].astype(f32)], axis=0).astype(bf16)
            sums = jnp.dot(stacked, slots_ref[r, 1], preferred_element_type=f32)
            total = sums[:8] + sums[8:16] + own_weight[span] * fresh[r, 1:2]
            sums_ref[8 * r : 8 * r + 8] = total / mass[span]
    done = jnp.concatenate([sums_ref[pl.ds(g, count, stride=8), :] for g in range(group)], axis=1).astype(bf16)
    for k in range(out_ref.shape[0]):
        out_ref[k] = done


def resid_kernel(partial_ref, *refs):
    packs, out_ref = refs[:-1], refs[-1]
    count, width = partial_ref.shape[1:]
    columns = width // len(packs)
    back = lax.rem(len(packs) - lax.axis_index("x"), len(packs)) * columns
    total = partial_ref[0]
    for k in range(1, partial_ref.shape[0]):
        total = total + partial_ref[k]
    squares = jnp.zeros((count, 1), f32)
    blocks = []
    for step, pack_ref in enumerate(packs):
        tail = pack_ref[columns:].astype(f32)
        gain = (tail[count : count + 1] + tail[count + 1 : count + 2] + tail[count + 2 : count + 3])[:, :columns]
        hidden = pltpu.roll(tail[:count], back, 1)[:, :columns]
        resid = total[:, step * columns : (step + 1) * columns] + hidden
        resid = resid.astype(bf16).astype(f32)
        squares = squares + jnp.sum(resid * resid, axis=1, keepdims=True)
        blocks.append(resid * gain)
    shift = lax.rem(lax.axis_index("x") + 1, len(packs)) * columns
    ordered = pltpu.roll(jnp.concatenate(blocks[::-1], axis=1), shift, 1)
    lane = lax.broadcasted_iota(jnp.int32, (count, LANES), 1)
    spare = jnp.zeros((count, LANES), f32)
    for k, part in enumerate(three_parts(squares)):
        spare = jnp.where(lane == k, part, spare)
    done = jnp.concatenate([ordered, spare], axis=1).astype(bf16)
    for k in range(out_ref.shape[0]):
        out_ref[k] = done


def norm_kernel(rows_ref, out_ref):
    blocks, count, padded = rows_ref.shape
    width = padded - LANES
    squares = jnp.zeros((count, LANES), f32)
    for k in range(blocks):
        squares = squares + rows_ref[k, :, width:].astype(f32)
    factor = lax.rsqrt(jnp.sum(squares, axis=1, keepdims=True) / D + epsilon)
    for k in range(blocks):
        done = (rows_ref[k, :, :width].astype(f32) * factor).astype(bf16)
        for copy in range(out_ref.shape[0]):
            out_ref[copy, :, k * width : (k + 1) * width] = done


def fetch_kernel(head_hbm, after_ref, head_ref, sem):
    load = pltpu.make_async_copy(head_hbm, head_ref, sem)
    load.start()
    load.wait()


def logits_kernel(head_ref, rows_ref, ids_ref, logits_ref, stats_ref):
    depth = head_ref.shape[1]
    for k in range(depth // CHUNK):
        span = slice(k * CHUNK, (k + 1) * CHUNK)
        product = lax.dot_general(
            head_ref[:, span], rows_ref[:, span], (((1,), (1,)), ((), ())), preferred_element_type=f32
        )
        if k == 0:
            logits_ref[...] = product
        else:
            logits_ref[...] += product
    logits = logits_ref[...]
    top = jnp.max(logits, axis=0, keepdims=True)
    log_mass = top + jnp.log(jnp.sum(jnp.exp(logits - top), axis=0, keepdims=True))
    hits = lax.broadcasted_iota(jnp.int32, logits.shape, 0) == ids_ref[...]
    picked = jnp.sum(jnp.where(hits, logits, 0.0), axis=0, keepdims=True)
    stats_ref[...] = jnp.concatenate([log_mass, picked], axis=0)


def final_kernel(logits_ref, stats_ref, mu_ref, logprobs_ref, surprise_ref, mu_next_ref):
    masses = stats_ref[:, 0]
    top = jnp.max(masses, axis=0, keepdims=True)
    log_mass = top + jnp.log(jnp.sum(jnp.exp(masses - top), axis=0, keepdims=True))
    picked = jnp.sum(stats_ref[:, 1], axis=0, keepdims=True)
    logprobs_ref[...] = logits_ref[...] - log_mass
    surprise = (log_mass - picked) / math.log(2.0)
    surprise_ref[...] = surprise
    mu_next_ref[...] = mu_ref[...] - learn_rate * (surprise - target_bits)


def spread(block, axes, count):
    many = jnp.broadcast_to(block[None], (count,) + block.shape)
    return lax.all_to_all(many, axes, split_axis=0, concat_axis=0, tiled=False)


def shards(query, cache, new_kv, lengths, hidden_in, out_proj, final_gain, lm_head, tokens, mu):
    nz, nx, ny, nc = (lax.axis_size(a) for a in ("z", "x", "y", "c"))
    z, x, y, c = (lax.axis_index(a) for a in ("z", "x", "y", "c"))
    count = query.shape[0]
    heads, columns = out_proj.shape
    sizes = {"z": nz, "x": nx, "y": ny, "c": nc}

    def from_along_x(block, step):
        return lax.ppermute(block, "x", [(i, (i + step) % nx) for i in range(nx)])

    pack = pl.pallas_call(
        functools.partial(pack_kernel, sizes),
        out_shape=jax.ShapeDtypeStruct((columns + TAIL, heads), bf16),
        in_specs=[IN_PLACE] * 3,
        out_specs=IN_PLACE,
        scratch_shapes=[
            pltpu.VMEM((columns, hidden_in.shape[0]), bf16),
            pltpu.VMEM((1, columns), f32),
            pltpu.VMEM((TAIL, heads), bf16),
            pltpu.SemaphoreType.DMA((4,)),
        ],
        compiler_params=WHOLE,
        name="pack",
    )(out_proj.T, hidden_in.T, final_gain[None])
    packs = [pack] + [from_along_x(pack, k) for k in range(1, nx)]
    table = jnp.concatenate([out_proj.T] + [p[:columns] for p in packs[1:]], axis=0)
    many = pl.pallas_call(
        functools.partial(attend_kernel, HEADS // KV_HEADS, sizes),
        out_shape=jax.ShapeDtypeStruct((nz,) + query.shape, bf16),
        in_specs=[IN_SMEM] + [IN_VMEM] * 2 + [IN_PLACE],
        out_specs=IN_VMEM,
        scratch_shapes=[
            pltpu.VMEM(cache.shape, bf16),
            pltpu.VMEM((count * 8, HEAD_DIM), f32),
            pltpu.VMEM((count * 8, HEAD_DIM), f32),
            pltpu.SemaphoreType.DMA((2, count)),
        ],
        compiler_params=WHOLE,
        name="attend",
    )(lengths, query, new_kv, cache)
    gathered = lax.all_to_all(many, "z", split_axis=0, concat_axis=0, tiled=False)
    gathered = gathered.reshape(nz * count, -1)
    partial = lax.dot_general(
        gathered, table, (((1,), (1,)), ((), ())), preferred_element_type=f32
    )
    partial = partial.reshape(nz, count, nx * columns)
    partial = lax.all_to_all(partial, ("c", "y"), split_axis=0, concat_axis=0, tiled=False)

    width = nx * columns
    rows = pl.pallas_call(
        resid_kernel,
        out_shape=jax.ShapeDtypeStruct((nz, count, width + LANES), bf16),
        in_specs=[IN_VMEM] * (nx + 1),
        out_specs=IN_VMEM,
        compiler_params=SMALL,
        name="resid",
    )(partial, *packs)
    rows = lax.all_to_all(rows, "z", split_axis=0, concat_axis=0, tiled=False)
    half = pl.pallas_call(
        norm_kernel,
        out_shape=jax.ShapeDtypeStruct((nx * ny, count, nz * width), bf16),
        in_specs=[IN_VMEM],
        out_specs=IN_VMEM,
        compiler_params=SMALL,
        name="norm",
    )(rows)
    half = lax.all_to_all(half, ("y", "x"), split_axis=0, concat_axis=0, tiled=False)
    half = half.reshape(ny * nx * count, -1)
    other = lax.ppermute(half, "c", [(i, 1 - i) for i in range(2)])
    head = pl.pallas_call(
        fetch_kernel,
        out_shape=jax.ShapeDtypeStruct(lm_head.shape, bf16),
        in_specs=[IN_PLACE] * 2,
        out_specs=IN_VMEM,
        scratch_shapes=[pltpu.SemaphoreType.DMA],
        compiler_params=WIDE,
        name="fetch",
    )(lm_head, half)
    other, head = lax.optimization_barrier((other, head))
    first = jnp.where(c == 0, half, other)
    second = jnp.where(c == 0, other, half)
    everyone = jnp.concatenate([first, second], axis=0)

    vocab = lm_head.shape[0]
    requests = everyone.shape[0]
    offset = (((z * nx + x) * ny + y) * nc + c) * vocab
    logits, stats = pl.pallas_call(
        logits_kernel,
        out_shape=[jax.ShapeDtypeStruct((vocab, requests), f32), jax.ShapeDtypeStruct((2, requests), f32)],
        in_specs=[IN_VMEM] * 3,
        out_specs=[IN_VMEM] * 2,
        compiler_params=SMALL,
        name="logits",
    )(head, everyone, (tokens - offset)[None])

    stats = spread(stats, ("x", "y", "c"), nx * ny * nc)
    top = jnp.max(stats[:, 0], axis=0)
    log_mass = top + jnp.log(jnp.sum(jnp.exp(stats[:, 0] - top[None, :]), axis=0))
    picked = jnp.sum(stats[:, 1], axis=0)
    stats = spread(jnp.stack([log_mass, picked]), "z", nz)
    row_shape = jax.ShapeDtypeStruct((1, requests), f32)
    logprobs, surprise, mu_next = pl.pallas_call(
        final_kernel,
        out_shape=[jax.ShapeDtypeStruct((vocab, requests), f32), row_shape, row_shape],
        in_specs=[IN_VMEM] * 3,
        out_specs=[IN_VMEM] * 3,
        compiler_params=SMALL,
        name="final",
    )(logits, stats, mu[None])
    return (logprobs.T, surprise[0], mu_next[0])


def solution(mesh):
    grid = Mesh(np.asarray(mesh.devices).reshape(8, 4, 4, 2), ("z", "x", "y", "c"))
    dp, tensor = ("z", "x"), ("y", "c")
    placed = (
        P(dp, tensor),
        P(dp, None, None, tensor),
        P(dp, None, tensor),
        P(),
        P(None, dp),
        P(tensor, dp),
        P(dp),
        P(dp + tensor, None),
        P(),
        P(),
    )
    return jax.shard_map(
        shards,
        mesh=grid,
        in_specs=placed,
        out_specs=(P(None, dp + tensor), P(), P()),
        check_vma=False,
    )
```

```python
import functools
import math

import jax
import jax.numpy as jnp
import numpy as np
from jax import lax
from jax.experimental import pallas as pl
from jax.experimental.pallas import tpu as pltpu
from jax.sharding import Mesh
from jax.sharding import PartitionSpec as P

D = 5120
HEADS = 40
KV_HEADS = 8
HEAD_DIM = 128

masked_score = -1e30
epsilon = 1e-06
learn_rate = 0.1
target_bits = 5.0

bf16 = jnp.bfloat16
f32 = jnp.float32
LANES = 128

IN_VMEM = pl.BlockSpec(memory_space=pltpu.VMEM)
IN_SMEM = pl.BlockSpec(memory_space=pltpu.SMEM)
IN_PLACE = pl.BlockSpec(memory_space=pl.ANY)
SMALL = pltpu.CompilerParams(vmem_limit_bytes=20 << 20)
WIDE = pltpu.CompilerParams(vmem_limit_bytes=44 << 20)
WHOLE = pltpu.CompilerParams(vmem_limit_bytes=60 << 20)
TAIL = 16
CHUNK = 1280


def three_parts(wide):
    first = wide.astype(bf16).astype(f32)
    rest = wide - first
    second = rest.astype(bf16).astype(f32)
    third = (rest - second).astype(bf16).astype(f32)
    return first, second, third


def side_by_side(rows):
    return jnp.concatenate([rows[k : k + 8] for k in range(0, rows.shape[0], 8)], axis=1)


def pack_kernel(sizes, table_hbm, hidden_hbm, gain_hbm, pack_ref, hidden_ref, gain_ref, sems):
    columns, heads = table_hbm.shape
    table = pltpu.make_async_copy(table_hbm, pack_ref.at[pl.ds(0, columns)], sems.at[0])
    hidden = pltpu.make_async_copy(hidden_hbm, hidden_ref, sems.at[1])
    gain = pltpu.make_async_copy(gain_hbm, gain_ref, sems.at[2])
    hidden.start()
    gain.start()
    table.start()
    rows, requests = heads // columns * 8, hidden_ref.shape[1]
    part = lax.axis_index("c") * sizes["y"] + lax.axis_index("y")
    row = lax.broadcasted_iota(jnp.int32, (rows, requests), 0)
    lane = lax.broadcasted_iota(jnp.int32, (rows, requests), 1)
    chosen = jnp.where(lane == row + part * rows, 1.0, 0.0).astype(bf16)
    hidden.wait()
    gain.wait()
    picked = lax.dot_general(
        chosen, hidden_ref[...], (((1,), (1,)), ((), ())), preferred_element_type=f32
    )
    below = jnp.concatenate(three_parts(gain_ref[...]) + (jnp.zeros((5, columns), f32),), axis=0)
    below = jnp.concatenate([below, jnp.zeros((8, heads - columns), f32)], axis=1)
    pack_ref[columns:] = jnp.concatenate([side_by_side(picked), below], axis=0).astype(bf16)
    table.wait()


def attend_kernel(group, sizes, lengths_ref, query_ref, new_ref, cache_ref, out_ref, slots_ref, rows_ref, sums_ref, sems):
    count, _, slots, head_dim = cache_ref.shape
    z, x = lax.axis_index("z"), lax.axis_index("x")
    scale = head_dim ** (-0.5)
    portions = [range(k, k + count // 2) for k in (0, count // 2)]
    loads = [
        [
            pltpu.make_async_copy(cache_ref.at[r, kind], slots_ref.at[r, kind], sems.at[kind, r])
            for r in portion
        ]
        for portion in portions
        for kind in range(2)
    ]
    for load in sum(loads, []):
        load.start()

    query = query_ref[...].astype(f32)
    fresh = new_ref[...].astype(f32)
    rows_ref[...] = jnp.zeros_like(rows_ref)
    for g in range(group):
        rows_ref[pl.ds(g, count, stride=8), :] = query[:, g * head_dim : (g + 1) * head_dim]
    heads = rows_ref[...]
    new_keys = jnp.concatenate([jnp.broadcast_to(fresh[r, 0:1], (8, head_dim)) for r in range(count)], axis=0)
    own_scores = jnp.sum(heads * new_keys, axis=1, keepdims=True) * scale
    heads = heads.astype(bf16)
    position = lax.broadcasted_iota(jnp.int32, (8, slots), 1)
    base = (z * sizes["x"] + x) * count
    for portion, key_loads, value_loads in zip(portions, loads[::2], loads[1::2]):
        for load in key_loads:
            load.wait()
        scores = []
        for r in portion:
            score = lax.dot_general(
                heads[8 * r : 8 * r + 8],
                slots_ref[r, 0],
                (((1,), (1,)), ((), ())),
                preferred_element_type=f32,
            )
            scores.append(jnp.where(position < lengths_ref[base + r], score * scale, masked_score))
        scores = jnp.concatenate(scores, axis=0)
        own_score = own_scores[8 * portion[0] : 8 * portion[0] + scores.shape[0]]
        top = jnp.maximum(jnp.max(scores, axis=1, keepdims=True), own_score)
        weights = jnp.exp(scores - top)
        own_weight = jnp.exp(own_score - top)
        mass = jnp.sum(weights, axis=1, keepdims=True) + own_weight
        coarse = weights.astype(bf16)
        fine = (weights - coarse.astype(f32)).astype(bf16)
        for load in value_loads:
            load.wait()
        for k, r in enumerate(portion):
            span = slice(8 * k, 8 * k + 8)
            stacked = jnp.concatenate([coarse[span].astype(f32), fine[span].astype(f32)], axis=0).astype(bf16)
            sums = jnp.dot(stacked, slots_ref[r, 1], preferred_element_type=f32)
            total = sums[:8] + sums[8:16] + own_weight[span] * fresh[r, 1:2]
            sums_ref[8 * r : 8 * r + 8] = total / mass[span]
    done = jnp.concatenate([sums_ref[pl.ds(g, count, stride=8), :] for g in range(group)], axis=1).astype(bf16)
    for k in range(out_ref.shape[0]):
        out_ref[k] = done


def resid_kernel(partial_ref, *refs):
    packs, out_ref = refs[:-1], refs[-1]
    count, width = partial_ref.shape[1:]
    columns = width // len(packs)
    back = lax.rem(len(packs) - lax.axis_index("x"), len(packs)) * columns
    total = partial_ref[0]
    for k in range(1, partial_ref.shape[0]):
        total = total + partial_ref[k]
    squares = jnp.zeros((count, 1), f32)
    blocks = []
    for step, pack_ref in enumerate(packs):
        tail = pack_ref[columns:].astype(f32)
        gain = (tail[count : count + 1] + tail[count + 1 : count + 2] + tail[count + 2 : count + 3])[:, :columns]
        hidden = pltpu.roll(tail[:count], back, 1)[:, :columns]
        resid = total[:, step * columns : (step + 1) * columns] + hidden
        resid = resid.astype(bf16).astype(f32)
        squares = squares + jnp.sum(resid * resid, axis=1, keepdims=True)
        blocks.append(resid * gain)
    shift = lax.rem(lax.axis_index("x") + 1, len(packs)) * columns
    ordered = pltpu.roll(jnp.concatenate(blocks[::-1], axis=1), shift, 1)
    lane = lax.broadcasted_iota(jnp.int32, (count, LANES), 1)
    spare = jnp.zeros((count, LANES), f32)
    for k, part in enumerate(three_parts(squares)):
        spare = jnp.where(lane == k, part, spare)
    done = jnp.concatenate([ordered, spare], axis=1).astype(bf16)
    for k in range(out_ref.shape[0]):
        out_ref[k] = done


def norm_kernel(rows_ref, out_ref):
    blocks, count, padded = rows_ref.shape
    width = padded - LANES
    squares = jnp.zeros((count, LANES), f32)
    for k in range(blocks):
        squares = squares + rows_ref[k, :, width:].astype(f32)
    factor = lax.rsqrt(jnp.sum(squares, axis=1, keepdims=True) / D + epsilon)
    for k in range(blocks):
        done = (rows_ref[k, :, :width].astype(f32) * factor).astype(bf16)
        for copy in range(out_ref.shape[0]):
            out_ref[copy, :, k * width : (k + 1) * width] = done


def fetch_kernel(head_hbm, after_ref, head_ref, sem):
    load = pltpu.make_async_copy(head_hbm, head_ref, sem)
    load.start()
    load.wait()


def logits_kernel(head_ref, rows_ref, ids_ref, logits_ref, stats_ref):
    depth = head_ref.shape[1]
    for k in range(depth // CHUNK):
        span = slice(k * CHUNK, (k + 1) * CHUNK)
        product = lax.dot_general(
            head_ref[:, span], rows_ref[:, span], (((1,), (1,)), ((), ())), preferred_element_type=f32
        )
        if k == 0:
            logits_ref[...] = product
        else:
            logits_ref[...] += product
    logits = logits_ref[...]
    top = jnp.max(logits, axis=0, keepdims=True)
    log_mass = top + jnp.log(jnp.sum(jnp.exp(logits - top), axis=0, keepdims=True))
    hits = lax.broadcasted_iota(jnp.int32, logits.shape, 0) == ids_ref[...]
    picked = jnp.sum(jnp.where(hits, logits, 0.0), axis=0, keepdims=True)
    stats_ref[...] = jnp.concatenate([log_mass, picked], axis=0)


def final_kernel(logits_ref, stats_ref, mu_ref, logprobs_ref, surprise_ref, mu_next_ref):
    masses = stats_ref[:, 0]
    top = jnp.max(masses, axis=0, keepdims=True)
    log_mass = top + jnp.log(jnp.sum(jnp.exp(masses - top), axis=0, keepdims=True))
    picked = jnp.sum(stats_ref[:, 1], axis=0, keepdims=True)
    logprobs_ref[...] = logits_ref[...] - log_mass
    surprise = (log_mass - picked) / math.log(2.0)
    surprise_ref[...] = surprise
    mu_next_ref[...] = mu_ref[...] - learn_rate * (surprise - target_bits)


def spread(block, axes, count):
    many = jnp.broadcast_to(block[None], (count,) + block.shape)
    return lax.all_to_all(many, axes, split_axis=0, concat_axis=0, tiled=False)


def shards(query, cache, new_kv, lengths, hidden_in, out_proj, final_gain, lm_head, tokens, mu):
    nz, nx, ny, nc = (lax.axis_size(a) for a in ("z", "x", "y", "c"))
    z, x, y, c = (lax.axis_index(a) for a in ("z", "x", "y", "c"))
    count = query.shape[0]
    heads, columns = out_proj.shape
    sizes = {"z": nz, "x": nx, "y": ny, "c": nc}

    def from_along_x(block, step):
        return lax.ppermute(block, "x", [(i, (i + step) % nx) for i in range(nx)])

    pack = pl.pallas_call(
        functools.partial(pack_kernel, sizes),
        out_shape=jax.ShapeDtypeStruct((columns + TAIL, heads), bf16),
        in_specs=[IN_PLACE] * 3,
        out_specs=IN_VMEM,
        scratch_shapes=[
            pltpu.VMEM((columns, hidden_in.shape[0]), bf16),
            pltpu.VMEM((1, columns), f32),
            pltpu.SemaphoreType.DMA((3,)),
        ],
        compiler_params=WHOLE,
        name="pack",
    )(out_proj.T, hidden_in.T, final_gain[None])
    packs = [pack] + [from_along_x(pack, k) for k in range(1, nx)]
    table = jnp.concatenate([out_proj.T] + [p[:columns] for p in packs[1:]], axis=0)
    many = pl.pallas_call(
        functools.partial(attend_kernel, HEADS // KV_HEADS, sizes),
        out_shape=jax.ShapeDtypeStruct((nz,) + query.shape, bf16),
        in_specs=[IN_SMEM] + [IN_VMEM] * 2 + [IN_PLACE],
        out_specs=IN_VMEM,
        scratch_shapes=[
            pltpu.VMEM(cache.shape, bf16),
            pltpu.VMEM((count * 8, HEAD_DIM), f32),
            pltpu.VMEM((count * 8, HEAD_DIM), f32),
            pltpu.SemaphoreType.DMA((2, count)),
        ],
        compiler_params=WHOLE,
        name="attend",
    )(lengths, query, new_kv, cache)
    gathered = lax.all_to_all(many, "z", split_axis=0, concat_axis=0, tiled=False)
    gathered = gathered.reshape(nz * count, -1)
    partial = lax.dot_general(
        gathered, table, (((1,), (1,)), ((), ())), preferred_element_type=f32
    )
    partial = partial.reshape(nz, count, nx * columns)
    partial = lax.all_to_all(partial, ("c", "y"), split_axis=0, concat_axis=0, tiled=False)

    width = nx * columns
    rows = pl.pallas_call(
        resid_kernel,
        out_shape=jax.ShapeDtypeStruct((nz, count, width + LANES), bf16),
        in_specs=[IN_VMEM] * (nx + 1),
        out_specs=IN_VMEM,
        compiler_params=SMALL,
        name="resid",
    )(partial, *packs)
    rows = lax.all_to_all(rows, "z", split_axis=0, concat_axis=0, tiled=False)
    half = pl.pallas_call(
        norm_kernel,
        out_shape=jax.ShapeDtypeStruct((nx * ny, count, nz * width), bf16),
        in_specs=[IN_VMEM],
        out_specs=IN_VMEM,
        compiler_params=SMALL,
        name="norm",
    )(rows)
    half = lax.all_to_all(half, ("y", "x"), split_axis=0, concat_axis=0, tiled=False)
    half = half.reshape(ny * nx * count, -1)
    other = lax.ppermute(half, "c", [(i, 1 - i) for i in range(2)])
    head = pl.pallas_call(
        fetch_kernel,
        out_shape=jax.ShapeDtypeStruct(lm_head.shape, bf16),
        in_specs=[IN_PLACE] * 2,
        out_specs=IN_VMEM,
        scratch_shapes=[pltpu.SemaphoreType.DMA],
        compiler_params=WIDE,
        name="fetch",
    )(lm_head, half)
    other, head = lax.optimization_barrier((other, head))
    first = jnp.where(c == 0, half, other)
    second = jnp.where(c == 0, other, half)
    everyone = jnp.concatenate([first, second], axis=0)

    vocab = lm_head.shape[0]
    requests = everyone.shape[0]
    offset = (((z * nx + x) * ny + y) * nc + c) * vocab
    logits, stats = pl.pallas_call(
        logits_kernel,
        out_shape=[jax.ShapeDtypeStruct((vocab, requests), f32), jax.ShapeDtypeStruct((2, requests), f32)],
        in_specs=[IN_VMEM] * 3,
        out_specs=[IN_VMEM] * 2,
        compiler_params=SMALL,
        name="logits",
    )(head, everyone, (tokens - offset)[None])

    stats = spread(stats, ("x", "y", "c"), nx * ny * nc)
    top = jnp.max(stats[:, 0], axis=0)
    log_mass = top + jnp.log(jnp.sum(jnp.exp(stats[:, 0] - top[None, :]), axis=0))
    picked = jnp.sum(stats[:, 1], axis=0)
    stats = spread(jnp.stack([log_mass, picked]), "z", nz)
    row_shape = jax.ShapeDtypeStruct((1, requests), f32)
    logprobs, surprise, mu_next = pl.pallas_call(
        final_kernel,
        out_shape=[jax.ShapeDtypeStruct((vocab, requests), f32), row_shape, row_shape],
        in_specs=[IN_VMEM] * 3,
        out_specs=[IN_VMEM] * 3,
        compiler_params=SMALL,
        name="final",
    )(logits, stats, mu[None])
    return (logprobs.T, surprise[0], mu_next[0])


def solution(mesh):
    grid = Mesh(np.asarray(mesh.devices).reshape(8, 4, 4, 2), ("z", "x", "y", "c"))
    dp, tensor = ("z", "x"), ("y", "c")
    placed = (
        P(dp, tensor),
        P(dp, None, None, tensor),
        P(dp, None, tensor),
        P(),
        P(None, dp),
        P(tensor, dp),
        P(dp),
        P(dp + tensor, None),
        P(),
        P(),
    )
    return jax.shard_map(
        shards,
        mesh=grid,
        in_specs=placed,
        out_specs=(P(None, dp + tensor), P(), P()),
        check_vma=False,
    )
```

```python
import functools
import math

import jax
import jax.numpy as jnp
import numpy as np
from jax import lax
from jax.experimental import pallas as pl
from jax.experimental.pallas import tpu as pltpu
from jax.sharding import Mesh
from jax.sharding import PartitionSpec as P

D = 5120
HEADS = 40
KV_HEADS = 8
HEAD_DIM = 128

masked_score = -1e30
epsilon = 1e-06
learn_rate = 0.1
target_bits = 5.0

bf16 = jnp.bfloat16
f32 = jnp.float32
LANES = 128

IN_VMEM = pl.BlockSpec(memory_space=pltpu.VMEM)
IN_SMEM = pl.BlockSpec(memory_space=pltpu.SMEM)
IN_PLACE = pl.BlockSpec(memory_space=pl.ANY)
SMALL = pltpu.CompilerParams(vmem_limit_bytes=20 << 20)
WIDE = pltpu.CompilerParams(vmem_limit_bytes=44 << 20)
WHOLE = pltpu.CompilerParams(vmem_limit_bytes=60 << 20)
TAIL = 16
CHUNK = 1280


def three_parts(wide):
    first = wide.astype(bf16).astype(f32)
    rest = wide - first
    second = rest.astype(bf16).astype(f32)
    third = (rest - second).astype(bf16).astype(f32)
    return first, second, third


def side_by_side(rows):
    return jnp.concatenate([rows[k : k + 8] for k in range(0, rows.shape[0], 8)], axis=1)


def pack_tail(sizes, hidden_ref, gain_ref, pack_ref):
    columns, requests = hidden_ref.shape
    heads = pack_ref.shape[1]
    rows = heads // columns * 8
    part = lax.axis_index("c") * sizes["y"] + lax.axis_index("y")
    row = lax.broadcasted_iota(jnp.int32, (rows, requests), 0)
    lane = lax.broadcasted_iota(jnp.int32, (rows, requests), 1)
    chosen = jnp.where(lane == row + part * rows, 1.0, 0.0).astype(bf16)
    picked = lax.dot_general(
        chosen, hidden_ref[...], (((1,), (1,)), ((), ())), preferred_element_type=f32
    )
    below = jnp.concatenate(three_parts(gain_ref[...]) + (jnp.zeros((5, columns), f32),), axis=0)
    below = jnp.concatenate([below, jnp.zeros((8, heads - columns), f32)], axis=1)
    pack_ref[columns:] = jnp.concatenate([side_by_side(picked), below], axis=0).astype(bf16)


def attend_kernel(group, sizes, lengths_ref, query_ref, new_ref, cache_ref, table_hbm, hidden_hbm, gain_hbm, *refs):
    out_ref, pack_ref, slots_ref, rows_ref, sums_ref, hidden_ref, gain_ref, sems, pack_sems = refs
    count, _, slots, head_dim = cache_ref.shape
    columns = table_hbm.shape[0]
    z, x = lax.axis_index("z"), lax.axis_index("x")
    scale = head_dim ** (-0.5)
    hidden = pltpu.make_async_copy(hidden_hbm, hidden_ref, pack_sems.at[0])
    gain = pltpu.make_async_copy(gain_hbm, gain_ref, pack_sems.at[1])
    table = pltpu.make_async_copy(table_hbm, pack_ref.at[pl.ds(0, columns)], pack_sems.at[2])
    portions = [range(k, k + count // 2) for k in (0, count // 2)]
    loads = [
        [
            pltpu.make_async_copy(cache_ref.at[r, kind], slots_ref.at[r, kind], sems.at[kind, r])
            for r in portion
        ]
        for portion in portions
        for kind in range(2)
    ]
    hidden.start()
    gain.start()
    for load in sum(loads, []):
        load.start()
    table.start()
    hidden.wait()
    gain.wait()
    pack_tail(sizes, hidden_ref, gain_ref, pack_ref)

    query = query_ref[...].astype(f32)
    fresh = new_ref[...].astype(f32)
    rows_ref[...] = jnp.zeros_like(rows_ref)
    for g in range(group):
        rows_ref[pl.ds(g, count, stride=8), :] = query[:, g * head_dim : (g + 1) * head_dim]
    heads = rows_ref[...]
    new_keys = jnp.concatenate([jnp.broadcast_to(fresh[r, 0:1], (8, head_dim)) for r in range(count)], axis=0)
    own_scores = jnp.sum(heads * new_keys, axis=1, keepdims=True) * scale
    heads = heads.astype(bf16)
    position = lax.broadcasted_iota(jnp.int32, (8, slots), 1)
    base = (z * sizes["x"] + x) * count
    for portion, key_loads, value_loads in zip(portions, loads[::2], loads[1::2]):
        for load in key_loads:
            load.wait()
        scores = []
        for r in portion:
            score = lax.dot_general(
                heads[8 * r : 8 * r + 8],
                slots_ref[r, 0],
                (((1,), (1,)), ((), ())),
                preferred_element_type=f32,
            )
            scores.append(jnp.where(position < lengths_ref[base + r], score * scale, masked_score))
        scores = jnp.concatenate(scores, axis=0)
        own_score = own_scores[8 * portion[0] : 8 * portion[0] + scores.shape[0]]
        top = jnp.maximum(jnp.max(scores, axis=1, keepdims=True), own_score)
        weights = jnp.exp(scores - top)
        own_weight = jnp.exp(own_score - top)
        mass = jnp.sum(weights, axis=1, keepdims=True) + own_weight
        coarse = weights.astype(bf16)
        fine = (weights - coarse.astype(f32)).astype(bf16)
        for load in value_loads:
            load.wait()
        for k, r in enumerate(portion):
            span = slice(8 * k, 8 * k + 8)
            stacked = jnp.concatenate([coarse[span].astype(f32), fine[span].astype(f32)], axis=0).astype(bf16)
            sums = jnp.dot(stacked, slots_ref[r, 1], preferred_element_type=f32)
            total = sums[:8] + sums[8:16] + own_weight[span] * fresh[r, 1:2]
            sums_ref[8 * r : 8 * r + 8] = total / mass[span]
    done = jnp.concatenate([sums_ref[pl.ds(g, count, stride=8), :] for g in range(group)], axis=1).astype(bf16)
    for k in range(out_ref.shape[0]):
        out_ref[k] = done
    table.wait()


def resid_kernel(partial_ref, *refs):
    packs, out_ref = refs[:-1], refs[-1]
    count, width = partial_ref.shape[1:]
    columns = width // len(packs)
    back = lax.rem(len(packs) - lax.axis_index("x"), len(packs)) * columns
    total = partial_ref[0]
    for k in range(1, partial_ref.shape[0]):
        total = total + partial_ref[k]
    squares = jnp.zeros((count, 1), f32)
    blocks = []
    for step, pack_ref in enumerate(packs):
        tail = pack_ref[columns:].astype(f32)
        gain = (tail[count : count + 1] + tail[count + 1 : count + 2] + tail[count + 2 : count + 3])[:, :columns]
        hidden = pltpu.roll(tail[:count], back, 1)[:, :columns]
        resid = total[:, step * columns : (step + 1) * columns] + hidden
        resid = resid.astype(bf16).astype(f32)
        squares = squares + jnp.sum(resid * resid, axis=1, keepdims=True)
        blocks.append(resid * gain)
    shift = lax.rem(lax.axis_index("x") + 1, len(packs)) * columns
    ordered = pltpu.roll(jnp.concatenate(blocks[::-1], axis=1), shift, 1)
    lane = lax.broadcasted_iota(jnp.int32, (count, LANES), 1)
    spare = jnp.zeros((count, LANES), f32)
    for k, part in enumerate(three_parts(squares)):
        spare = jnp.where(lane == k, part, spare)
    done = jnp.concatenate([ordered, spare], axis=1).astype(bf16)
    for k in range(out_ref.shape[0]):
        out_ref[k] = done


def norm_kernel(rows_ref, out_ref):
    blocks, count, padded = rows_ref.shape
    width = padded - LANES
    squares = jnp.zeros((count, LANES), f32)
    for k in range(blocks):
        squares = squares + rows_ref[k, :, width:].astype(f32)
    factor = lax.rsqrt(jnp.sum(squares, axis=1, keepdims=True) / D + epsilon)
    for k in range(blocks):
        done = (rows_ref[k, :, :width].astype(f32) * factor).astype(bf16)
        for copy in range(out_ref.shape[0]):
            out_ref[copy, :, k * width : (k + 1) * width] = done


def fetch_kernel(head_hbm, after_ref, head_ref, sem):
    load = pltpu.make_async_copy(head_hbm, head_ref, sem)
    load.start()
    load.wait()


def logits_kernel(head_ref, rows_ref, ids_ref, logits_ref, stats_ref):
    depth = head_ref.shape[1]
    for k in range(depth // CHUNK):
        span = slice(k * CHUNK, (k + 1) * CHUNK)
        product = lax.dot_general(
            head_ref[:, span], rows_ref[:, span], (((1,), (1,)), ((), ())), preferred_element_type=f32
        )
        if k == 0:
            logits_ref[...] = product
        else:
            logits_ref[...] += product
    logits = logits_ref[...]
    top = jnp.max(logits, axis=0, keepdims=True)
    log_mass = top + jnp.log(jnp.sum(jnp.exp(logits - top), axis=0, keepdims=True))
    hits = lax.broadcasted_iota(jnp.int32, logits.shape, 0) == ids_ref[...]
    picked = jnp.sum(jnp.where(hits, logits, 0.0), axis=0, keepdims=True)
    stats_ref[...] = jnp.concatenate([log_mass, picked], axis=0)


def final_kernel(logits_ref, stats_ref, mu_ref, logprobs_ref, surprise_ref, mu_next_ref):
    masses = stats_ref[:, 0]
    top = jnp.max(masses, axis=0, keepdims=True)
    log_mass = top + jnp.log(jnp.sum(jnp.exp(masses - top), axis=0, keepdims=True))
    picked = jnp.sum(stats_ref[:, 1], axis=0, keepdims=True)
    logprobs_ref[...] = logits_ref[...] - log_mass
    surprise = (log_mass - picked) / math.log(2.0)
    surprise_ref[...] = surprise
    mu_next_ref[...] = mu_ref[...] - learn_rate * (surprise - target_bits)


def spread(block, axes, count):
    many = jnp.broadcast_to(block[None], (count,) + block.shape)
    return lax.all_to_all(many, axes, split_axis=0, concat_axis=0, tiled=False)


def shards(query, cache, new_kv, lengths, hidden_in, out_proj, final_gain, lm_head, tokens, mu):
    nz, nx, ny, nc = (lax.axis_size(a) for a in ("z", "x", "y", "c"))
    z, x, y, c = (lax.axis_index(a) for a in ("z", "x", "y", "c"))
    count = query.shape[0]
    heads, columns = out_proj.shape
    sizes = {"z": nz, "x": nx, "y": ny, "c": nc}

    def from_along_x(block, step):
        return lax.ppermute(block, "x", [(i, (i + step) % nx) for i in range(nx)])

    many, pack = pl.pallas_call(
        functools.partial(attend_kernel, HEADS // KV_HEADS, sizes),
        out_shape=[
            jax.ShapeDtypeStruct((nz,) + query.shape, bf16),
            jax.ShapeDtypeStruct((columns + TAIL, heads), bf16),
        ],
        in_specs=[IN_SMEM] + [IN_VMEM] * 2 + [IN_PLACE] * 4,
        out_specs=[IN_VMEM] * 2,
        scratch_shapes=[
            pltpu.VMEM(cache.shape, bf16),
            pltpu.VMEM((count * 8, HEAD_DIM), f32),
            pltpu.VMEM((count * 8, HEAD_DIM), f32),
            pltpu.VMEM((columns, hidden_in.shape[0]), bf16),
            pltpu.VMEM((1, columns), f32),
            pltpu.SemaphoreType.DMA((2, count)),
            pltpu.SemaphoreType.DMA((3,)),
        ],
        compiler_params=WHOLE,
        name="attend",
    )(lengths, query, new_kv, cache, out_proj.T, hidden_in.T, final_gain[None])
    packs = [pack] + [from_along_x(pack, k) for k in range(1, nx)]
    table = jnp.concatenate([out_proj.T] + [p[:columns] for p in packs[1:]], axis=0)
    gathered = lax.all_to_all(many, "z", split_axis=0, concat_axis=0, tiled=False)
    gathered = gathered.reshape(nz * count, -1)
    partial = lax.dot_general(
        gathered, table, (((1,), (1,)), ((), ())), preferred_element_type=f32
    )
    partial = partial.reshape(nz, count, nx * columns)
    partial = lax.all_to_all(partial, ("c", "y"), split_axis=0, concat_axis=0, tiled=False)

    width = nx * columns
    rows = pl.pallas_call(
        resid_kernel,
        out_shape=jax.ShapeDtypeStruct((nz, count, width + LANES), bf16),
        in_specs=[IN_VMEM] * (nx + 1),
        out_specs=IN_VMEM,
        compiler_params=SMALL,
        name="resid",
    )(partial, *packs)
    rows = lax.all_to_all(rows, "z", split_axis=0, concat_axis=0, tiled=False)
    half = pl.pallas_call(
        norm_kernel,
        out_shape=jax.ShapeDtypeStruct((nx * ny, count, nz * width), bf16),
        in_specs=[IN_VMEM],
        out_specs=IN_VMEM,
        compiler_params=SMALL,
        name="norm",
    )(rows)
    half = lax.all_to_all(half, ("y", "x"), split_axis=0, concat_axis=0, tiled=False)
    half = half.reshape(ny * nx * count, -1)
    other = lax.ppermute(half, "c", [(i, 1 - i) for i in range(2)])
    head = pl.pallas_call(
        fetch_kernel,
        out_shape=jax.ShapeDtypeStruct(lm_head.shape, bf16),
        in_specs=[IN_PLACE] * 2,
        out_specs=IN_VMEM,
        scratch_shapes=[pltpu.SemaphoreType.DMA],
        compiler_params=WIDE,
        name="fetch",
    )(lm_head, half)
    other, head = lax.optimization_barrier((other, head))
    first = jnp.where(c == 0, half, other)
    second = jnp.where(c == 0, other, half)
    everyone = jnp.concatenate([first, second], axis=0)

    vocab = lm_head.shape[0]
    requests = everyone.shape[0]
    offset = (((z * nx + x) * ny + y) * nc + c) * vocab
    logits, stats = pl.pallas_call(
        logits_kernel,
        out_shape=[jax.ShapeDtypeStruct((vocab, requests), f32), jax.ShapeDtypeStruct((2, requests), f32)],
        in_specs=[IN_VMEM] * 3,
        out_specs=[IN_VMEM] * 2,
        compiler_params=SMALL,
        name="logits",
    )(head, everyone, (tokens - offset)[None])

    stats = spread(stats, ("x", "y", "c"), nx * ny * nc)
    top = jnp.max(stats[:, 0], axis=0)
    log_mass = top + jnp.log(jnp.sum(jnp.exp(stats[:, 0] - top[None, :]), axis=0))
    picked = jnp.sum(stats[:, 1], axis=0)
    stats = spread(jnp.stack([log_mass, picked]), "z", nz)
    row_shape = jax.ShapeDtypeStruct((1, requests), f32)
    logprobs, surprise, mu_next = pl.pallas_call(
        final_kernel,
        out_shape=[jax.ShapeDtypeStruct((vocab, requests), f32), row_shape, row_shape],
        in_specs=[IN_VMEM] * 3,
        out_specs=[IN_VMEM] * 3,
        compiler_params=SMALL,
        name="final",
    )(logits, stats, mu[None])
    return (logprobs.T, surprise[0], mu_next[0])


def solution(mesh):
    grid = Mesh(np.asarray(mesh.devices).reshape(8, 4, 4, 2), ("z", "x", "y", "c"))
    dp, tensor = ("z", "x"), ("y", "c")
    placed = (
        P(dp, tensor),
        P(dp, None, None, tensor),
        P(dp, None, tensor),
        P(),
        P(None, dp),
        P(tensor, dp),
        P(dp),
        P(dp + tensor, None),
        P(),
        P(),
    )
    return jax.shard_map(
        shards,
        mesh=grid,
        in_specs=placed,
        out_specs=(P(None, dp + tensor), P(), P()),
        check_vma=False,
    )
```

```python
import functools
import math

import jax
import jax.numpy as jnp
import numpy as np
from jax import lax
from jax.experimental import pallas as pl
from jax.experimental.pallas import tpu as pltpu
from jax.sharding import Mesh
from jax.sharding import PartitionSpec as P

D = 5120
HEADS = 40
KV_HEADS = 8
HEAD_DIM = 128

masked_score = -1e30
epsilon = 1e-06
learn_rate = 0.1
target_bits = 5.0

bf16 = jnp.bfloat16
f32 = jnp.float32
LANES = 128

IN_VMEM = pl.BlockSpec(memory_space=pltpu.VMEM)
IN_SMEM = pl.BlockSpec(memory_space=pltpu.SMEM)
IN_PLACE = pl.BlockSpec(memory_space=pl.ANY)
SMALL = pltpu.CompilerParams(vmem_limit_bytes=20 << 20)
WIDE = pltpu.CompilerParams(vmem_limit_bytes=44 << 20)
WHOLE = pltpu.CompilerParams(vmem_limit_bytes=60 << 20)
TAIL = 16
CHUNK = 1280


def three_parts(wide):
    first = wide.astype(bf16).astype(f32)
    rest = wide - first
    second = rest.astype(bf16).astype(f32)
    third = (rest - second).astype(bf16).astype(f32)
    return first, second, third


def side_by_side(rows):
    return jnp.concatenate([rows[k : k + 8] for k in range(0, rows.shape[0], 8)], axis=1)


def pack_tail(sizes, hidden_ref, gain_ref, pack_ref):
    columns, requests = hidden_ref.shape
    heads = pack_ref.shape[1]
    rows = heads // columns * 8
    part = lax.axis_index("c") * sizes["y"] + lax.axis_index("y")
    row = lax.broadcasted_iota(jnp.int32, (rows, requests), 0)
    lane = lax.broadcasted_iota(jnp.int32, (rows, requests), 1)
    chosen = jnp.where(lane == row + part * rows, 1.0, 0.0).astype(bf16)
    picked = lax.dot_general(
        chosen, hidden_ref[...], (((1,), (1,)), ((), ())), preferred_element_type=f32
    )
    below = jnp.concatenate(three_parts(gain_ref[...]) + (jnp.zeros((5, columns), f32),), axis=0)
    below = jnp.concatenate([below, jnp.zeros((8, heads - columns), f32)], axis=1)
    pack_ref[columns:] = jnp.concatenate([side_by_side(picked), below], axis=0).astype(bf16)


def attend_kernel(group, sizes, lengths_ref, query_ref, new_ref, cache_ref, table_hbm, hidden_hbm, gain_hbm, *refs):
    out_ref, pack_ref, slots_ref, rows_ref, sums_ref, hidden_ref, gain_ref, sems, pack_sems = refs
    count, _, slots, head_dim = cache_ref.shape
    columns = table_hbm.shape[0]
    z, x = lax.axis_index("z"), lax.axis_index("x")
    scale = head_dim ** (-0.5)
    hidden = pltpu.make_async_copy(hidden_hbm, hidden_ref, pack_sems.at[0])
    gain = pltpu.make_async_copy(gain_hbm, gain_ref, pack_sems.at[1])
    table = pltpu.make_async_copy(table_hbm, pack_ref.at[pl.ds(0, columns)], pack_sems.at[2])
    portions = [range(k, k + count // 2) for k in (0, count // 2)]
    loads = [
        [
            pltpu.make_async_copy(cache_ref.at[r, kind], slots_ref.at[r, kind], sems.at[kind, r])
            for r in portion
        ]
        for portion in portions
        for kind in range(2)
    ]
    hidden.start()
    gain.start()
    for load in sum(loads, []):
        load.start()
    table.start()
    hidden.wait()
    gain.wait()
    pack_tail(sizes, hidden_ref, gain_ref, pack_ref)

    query = query_ref[...].astype(f32)
    fresh = new_ref[...].astype(f32)
    rows_ref[...] = jnp.zeros_like(rows_ref)
    for g in range(group):
        rows_ref[pl.ds(g, count, stride=8), :] = query[:, g * head_dim : (g + 1) * head_dim]
    heads = rows_ref[...]
    new_keys = jnp.concatenate([jnp.broadcast_to(fresh[r, 0:1], (8, head_dim)) for r in range(count)], axis=0)
    own_scores = jnp.sum(heads * new_keys, axis=1, keepdims=True) * scale
    position = lax.broadcasted_iota(jnp.int32, (16, slots), 1)
    upper_slots = lax.broadcasted_iota(jnp.int32, (16, slots), 0) < 8
    base = (z * sizes["x"] + x) * count
    for portion, key_loads, value_loads in zip(portions, loads[::2], loads[1::2]):
        for load in key_loads:
            load.wait()
        scores = []
        for r in portion[::2]:
            rows = heads[8 * r : 8 * r + 16]
            upper = lax.broadcasted_iota(jnp.int32, rows.shape, 0) < 8
            rows = jnp.concatenate([jnp.where(upper, rows, 0.0), jnp.where(upper, 0.0, rows)], axis=1)
            keys = jnp.concatenate([slots_ref[r, 0], slots_ref[r + 1, 0]], axis=1)
            score = lax.dot_general(
                rows.astype(bf16), keys, (((1,), (1,)), ((), ())), preferred_element_type=f32
            )
            live = jnp.where(upper_slots, lengths_ref[base + r], lengths_ref[base + r + 1])
            scores.append(jnp.where(position < live, score * scale, masked_score))
        scores = jnp.concatenate(scores, axis=0)
        own_score = own_scores[8 * portion[0] : 8 * portion[0] + scores.shape[0]]
        top = jnp.maximum(jnp.max(scores, axis=1, keepdims=True), own_score)
        weights = jnp.exp(scores - top)
        own_weight = jnp.exp(own_score - top)
        mass = jnp.sum(weights, axis=1, keepdims=True) + own_weight
        coarse = weights.astype(bf16)
        fine = (weights - coarse.astype(f32)).astype(bf16)
        for load in value_loads:
            load.wait()
        for k, r in zip(range(0, len(portion), 2), portion[::2]):
            span = slice(8 * k, 8 * k + 16)
            stacked = jnp.concatenate([coarse[span], fine[span]], axis=0)
            values = jnp.concatenate([slots_ref[r, 1], slots_ref[r + 1, 1]], axis=1)
            sums = jnp.dot(stacked, values, preferred_element_type=f32)
            sums = sums[:16] + sums[16:]
            for i in range(2):
                mine = slice(8 * (k + i), 8 * (k + i) + 8)
                total = sums[8 * i : 8 * i + 8, i * head_dim : (i + 1) * head_dim]
                total = total + own_weight[mine] * fresh[r + i, 1:2]
                sums_ref[8 * (r + i) : 8 * (r + i) + 8] = total / mass[mine]
    done = jnp.concatenate([sums_ref[pl.ds(g, count, stride=8), :] for g in range(group)], axis=1).astype(bf16)
    for k in range(out_ref.shape[0]):
        out_ref[k] = done
    table.wait()


def resid_kernel(partial_ref, *refs):
    packs, out_ref = refs[:-1], refs[-1]
    count, width = partial_ref.shape[1:]
    columns = width // len(packs)
    back = lax.rem(len(packs) - lax.axis_index("x"), len(packs)) * columns
    total = partial_ref[0]
    for k in range(1, partial_ref.shape[0]):
        total = total + partial_ref[k]
    squares = jnp.zeros((count, 1), f32)
    blocks = []
    for step, pack_ref in enumerate(packs):
        tail = pack_ref[columns:].astype(f32)
        gain = (tail[count : count + 1] + tail[count + 1 : count + 2] + tail[count + 2 : count + 3])[:, :columns]
        hidden = pltpu.roll(tail[:count], back, 1)[:, :columns]
        resid = total[:, step * columns : (step + 1) * columns] + hidden
        resid = resid.astype(bf16).astype(f32)
        squares = squares + jnp.sum(resid * resid, axis=1, keepdims=True)
        blocks.append(resid * gain)
    shift = lax.rem(lax.axis_index("x") + 1, len(packs)) * columns
    ordered = pltpu.roll(jnp.concatenate(blocks[::-1], axis=1), shift, 1)
    lane = lax.broadcasted_iota(jnp.int32, (count, LANES), 1)
    spare = jnp.zeros((count, LANES), f32)
    for k, part in enumerate(three_parts(squares)):
        spare = jnp.where(lane == k, part, spare)
    done = jnp.concatenate([ordered, spare], axis=1).astype(bf16)
    for k in range(out_ref.shape[0]):
        out_ref[k] = done


def norm_kernel(rows_ref, out_ref):
    blocks, count, padded = rows_ref.shape
    width = padded - LANES
    squares = jnp.zeros((count, LANES), f32)
    for k in range(blocks):
        squares = squares + rows_ref[k, :, width:].astype(f32)
    factor = lax.rsqrt(jnp.sum(squares, axis=1, keepdims=True) / D + epsilon)
    for k in range(blocks):
        done = (rows_ref[k, :, :width].astype(f32) * factor).astype(bf16)
        for copy in range(out_ref.shape[0]):
            out_ref[copy, :, k * width : (k + 1) * width] = done


def fetch_kernel(head_hbm, after_ref, head_ref, sem):
    load = pltpu.make_async_copy(head_hbm, head_ref, sem)
    load.start()
    load.wait()


def logits_kernel(head_ref, rows_ref, ids_ref, logits_ref, stats_ref):
    depth = head_ref.shape[1]
    for k in range(depth // CHUNK):
        span = slice(k * CHUNK, (k + 1) * CHUNK)
        product = lax.dot_general(
            head_ref[:, span], rows_ref[:, span], (((1,), (1,)), ((), ())), preferred_element_type=f32
        )
        if k == 0:
            logits_ref[...] = product
        else:
            logits_ref[...] += product
    logits = logits_ref[...]
    top = jnp.max(logits, axis=0, keepdims=True)
    log_mass = top + jnp.log(jnp.sum(jnp.exp(logits - top), axis=0, keepdims=True))
    hits = lax.broadcasted_iota(jnp.int32, logits.shape, 0) == ids_ref[...]
    picked = jnp.sum(jnp.where(hits, logits, 0.0), axis=0, keepdims=True)
    stats_ref[...] = jnp.concatenate([log_mass, picked], axis=0)


def final_kernel(logits_ref, stats_ref, mu_ref, logprobs_ref, surprise_ref, mu_next_ref):
    masses = stats_ref[:, 0]
    top = jnp.max(masses, axis=0, keepdims=True)
    log_mass = top + jnp.log(jnp.sum(jnp.exp(masses - top), axis=0, keepdims=True))
    picked = jnp.sum(stats_ref[:, 1], axis=0, keepdims=True)
    logprobs_ref[...] = logits_ref[...] - log_mass
    surprise = (log_mass - picked) / math.log(2.0)
    surprise_ref[...] = surprise
    mu_next_ref[...] = mu_ref[...] - learn_rate * (surprise - target_bits)


def spread(block, axes, count):
    many = jnp.broadcast_to(block[None], (count,) + block.shape)
    return lax.all_to_all(many, axes, split_axis=0, concat_axis=0, tiled=False)


def shards(query, cache, new_kv, lengths, hidden_in, out_proj, final_gain, lm_head, tokens, mu):
    nz, nx, ny, nc = (lax.axis_size(a) for a in ("z", "x", "y", "c"))
    z, x, y, c = (lax.axis_index(a) for a in ("z", "x", "y", "c"))
    count = query.shape[0]
    heads, columns = out_proj.shape
    sizes = {"z": nz, "x": nx, "y": ny, "c": nc}

    def from_along_x(block, step):
        return lax.ppermute(block, "x", [(i, (i + step) % nx) for i in range(nx)])

    many, pack = pl.pallas_call(
        functools.partial(attend_kernel, HEADS // KV_HEADS, sizes),
        out_shape=[
            jax.ShapeDtypeStruct((nz,) + query.shape, bf16),
            jax.ShapeDtypeStruct((columns + TAIL, heads), bf16),
        ],
        in_specs=[IN_SMEM] + [IN_VMEM] * 2 + [IN_PLACE] * 4,
        out_specs=[IN_VMEM] * 2,
        scratch_shapes=[
            pltpu.VMEM(cache.shape, bf16),
            pltpu.VMEM((count * 8, HEAD_DIM), f32),
            pltpu.VMEM((count * 8, HEAD_DIM), f32),
            pltpu.VMEM((columns, hidden_in.shape[0]), bf16),
            pltpu.VMEM((1, columns), f32),
            pltpu.SemaphoreType.DMA((2, count)),
            pltpu.SemaphoreType.DMA((3,)),
        ],
        compiler_params=WHOLE,
        name="attend",
    )(lengths, query, new_kv, cache, out_proj.T, hidden_in.T, final_gain[None])
    packs = [pack] + [from_along_x(pack, k) for k in range(1, nx)]
    table = jnp.concatenate([out_proj.T] + [p[:columns] for p in packs[1:]], axis=0)
    gathered = lax.all_to_all(many, "z", split_axis=0, concat_axis=0, tiled=False)
    gathered = gathered.reshape(nz * count, -1)
    partial = lax.dot_general(
        gathered, table, (((1,), (1,)), ((), ())), preferred_element_type=f32
    )
    partial = partial.reshape(nz, count, nx * columns)
    partial = lax.all_to_all(partial, ("c", "y"), split_axis=0, concat_axis=0, tiled=False)

    width = nx * columns
    rows = pl.pallas_call(
        resid_kernel,
        out_shape=jax.ShapeDtypeStruct((nz, count, width + LANES), bf16),
        in_specs=[IN_VMEM] * (nx + 1),
        out_specs=IN_VMEM,
        compiler_params=SMALL,
        name="resid",
    )(partial, *packs)
    rows = lax.all_to_all(rows, "z", split_axis=0, concat_axis=0, tiled=False)
    half = pl.pallas_call(
        norm_kernel,
        out_shape=jax.ShapeDtypeStruct((nx * ny, count, nz * width), bf16),
        in_specs=[IN_VMEM],
        out_specs=IN_VMEM,
        compiler_params=SMALL,
        name="norm",
    )(rows)
    half = lax.all_to_all(half, ("y", "x"), split_axis=0, concat_axis=0, tiled=False)
    half = half.reshape(ny * nx * count, -1)
    other = lax.ppermute(half, "c", [(i, 1 - i) for i in range(2)])
    head = pl.pallas_call(
        fetch_kernel,
        out_shape=jax.ShapeDtypeStruct(lm_head.shape, bf16),
        in_specs=[IN_PLACE] * 2,
        out_specs=IN_VMEM,
        scratch_shapes=[pltpu.SemaphoreType.DMA],
        compiler_params=WIDE,
        name="fetch",
    )(lm_head, half)
    other, head = lax.optimization_barrier((other, head))
    first = jnp.where(c == 0, half, other)
    second = jnp.where(c == 0, other, half)
    everyone = jnp.concatenate([first, second], axis=0)

    vocab = lm_head.shape[0]
    requests = everyone.shape[0]
    offset = (((z * nx + x) * ny + y) * nc + c) * vocab
    logits, stats = pl.pallas_call(
        logits_kernel,
        out_shape=[jax.ShapeDtypeStruct((vocab, requests), f32), jax.ShapeDtypeStruct((2, requests), f32)],
        in_specs=[IN_VMEM] * 3,
        out_specs=[IN_VMEM] * 2,
        compiler_params=SMALL,
        name="logits",
    )(head, everyone, (tokens - offset)[None])

    stats = spread(stats, ("x", "y", "c"), nx * ny * nc)
    top = jnp.max(stats[:, 0], axis=0)
    log_mass = top + jnp.log(jnp.sum(jnp.exp(stats[:, 0] - top[None, :]), axis=0))
    picked = jnp.sum(stats[:, 1], axis=0)
    stats = spread(jnp.stack([log_mass, picked]), "z", nz)
    row_shape = jax.ShapeDtypeStruct((1, requests), f32)
    logprobs, surprise, mu_next = pl.pallas_call(
        final_kernel,
        out_shape=[jax.ShapeDtypeStruct((vocab, requests), f32), row_shape, row_shape],
        in_specs=[IN_VMEM] * 3,
        out_specs=[IN_VMEM] * 3,
        compiler_params=SMALL,
        name="final",
    )(logits, stats, mu[None])
    return (logprobs.T, surprise[0], mu_next[0])


def solution(mesh):
    grid = Mesh(np.asarray(mesh.devices).reshape(8, 4, 4, 2), ("z", "x", "y", "c"))
    dp, tensor = ("z", "x"), ("y", "c")
    placed = (
        P(dp, tensor),
        P(dp, None, None, tensor),
        P(dp, None, tensor),
        P(),
        P(None, dp),
        P(tensor, dp),
        P(dp),
        P(dp + tensor, None),
        P(),
        P(),
    )
    return jax.shard_map(
        shards,
        mesh=grid,
        in_specs=placed,
        out_specs=(P(None, dp + tensor), P(), P()),
        check_vma=False,
    )
```

```python
import functools
import math

import jax
import jax.numpy as jnp
import numpy as np
from jax import lax
from jax.experimental import pallas as pl
from jax.experimental.pallas import tpu as pltpu
from jax.sharding import Mesh
from jax.sharding import PartitionSpec as P

D = 5120
HEADS = 40
KV_HEADS = 8
HEAD_DIM = 128

masked_score = -1e30
epsilon = 1e-06
learn_rate = 0.1
target_bits = 5.0

bf16 = jnp.bfloat16
f32 = jnp.float32
LANES = 128

IN_VMEM = pl.BlockSpec(memory_space=pltpu.VMEM)
IN_SMEM = pl.BlockSpec(memory_space=pltpu.SMEM)
IN_PLACE = pl.BlockSpec(memory_space=pl.ANY)
SMALL = pltpu.CompilerParams(vmem_limit_bytes=20 << 20)
WIDE = pltpu.CompilerParams(vmem_limit_bytes=44 << 20)
WHOLE = pltpu.CompilerParams(vmem_limit_bytes=60 << 20)
TAIL = 16
CHUNK = 1280


def three_parts(wide):
    first = wide.astype(bf16).astype(f32)
    rest = wide - first
    second = rest.astype(bf16).astype(f32)
    third = (rest - second).astype(bf16).astype(f32)
    return first, second, third


def side_by_side(rows):
    return jnp.concatenate([rows[k : k + 8] for k in range(0, rows.shape[0], 8)], axis=1)


def pack_tail(sizes, hidden_ref, gain_ref, pack_ref):
    columns, requests = hidden_ref.shape
    heads = pack_ref.shape[1]
    rows = heads // columns * 8
    part = lax.axis_index("c") * sizes["y"] + lax.axis_index("y")
    row = lax.broadcasted_iota(jnp.int32, (rows, requests), 0)
    lane = lax.broadcasted_iota(jnp.int32, (rows, requests), 1)
    chosen = jnp.where(lane == row + part * rows, 1.0, 0.0).astype(bf16)
    picked = lax.dot_general(
        chosen, hidden_ref[...], (((1,), (1,)), ((), ())), preferred_element_type=f32
    )
    below = jnp.concatenate(three_parts(gain_ref[...]) + (jnp.zeros((5, columns), f32),), axis=0)
    below = jnp.concatenate([below, jnp.zeros((8, heads - columns), f32)], axis=1)
    pack_ref[columns:] = jnp.concatenate([side_by_side(picked), below], axis=0).astype(bf16)


def attend_kernel(group, sizes, lengths_ref, query_hbm, new_hbm, cache_ref, table_hbm, hidden_hbm, gain_hbm, *refs):
    out_ref, pack_hbm, slots_ref, rows_ref, sums_ref, query_ref, new_ref, hidden_ref, gain_ref, pack_ref = refs[:-2]
    sems, small_sems = refs[-2:]
    count, _, slots, head_dim = cache_ref.shape
    columns = table_hbm.shape[0]
    z, x = lax.axis_index("z"), lax.axis_index("x")
    scale = head_dim ** (-0.5)
    small = [
        pltpu.make_async_copy(source, target, small_sems.at[k])
        for k, (source, target) in enumerate(
            (
                (query_hbm, query_ref),
                (new_hbm, new_ref),
                (hidden_hbm, hidden_ref),
                (gain_hbm, gain_ref),
                (table_hbm, pack_ref.at[pl.ds(0, columns)]),
            )
        )
    ]
    leave = pltpu.make_async_copy(pack_ref, pack_hbm, small_sems.at[len(small)])
    portions = [range(k, k + count // 2) for k in (0, count // 2)]
    loads = [
        [
            pltpu.make_async_copy(cache_ref.at[r, kind], slots_ref.at[r, kind], sems.at[kind, r])
            for r in portion
        ]
        for portion in portions
        for kind in range(2)
    ]
    for load in small + sum(loads, []):
        load.start()
    for load in small:
        load.wait()
    pack_tail(sizes, hidden_ref, gain_ref, pack_ref)
    leave.start()

    query = query_ref[...].astype(f32)
    fresh = new_ref[...].astype(f32)
    rows_ref[...] = jnp.zeros_like(rows_ref)
    for g in range(group):
        rows_ref[pl.ds(g, count, stride=8), :] = query[:, g * head_dim : (g + 1) * head_dim]
    heads = rows_ref[...]
    new_keys = jnp.concatenate([jnp.broadcast_to(fresh[r, 0:1], (8, head_dim)) for r in range(count)], axis=0)
    own_scores = jnp.sum(heads * new_keys, axis=1, keepdims=True) * scale
    heads = heads.astype(bf16)
    position = lax.broadcasted_iota(jnp.int32, (8, slots), 1)
    base = (z * sizes["x"] + x) * count
    for portion, key_loads, value_loads in zip(portions, loads[::2], loads[1::2]):
        for load in key_loads:
            load.wait()
        scores = []
        for r in portion:
            score = lax.dot_general(
                heads[8 * r : 8 * r + 8],
                slots_ref[r, 0],
                (((1,), (1,)), ((), ())),
                preferred_element_type=f32,
            )
            scores.append(jnp.where(position < lengths_ref[base + r], score * scale, masked_score))
        scores = jnp.concatenate(scores, axis=0)
        own_score = own_scores[8 * portion[0] : 8 * portion[0] + scores.shape[0]]
        top = jnp.maximum(jnp.max(scores, axis=1, keepdims=True), own_score)
        weights = jnp.exp(scores - top)
        own_weight = jnp.exp(own_score - top)
        mass = jnp.sum(weights, axis=1, keepdims=True) + own_weight
        coarse = weights.astype(bf16)
        fine = (weights - coarse.astype(f32)).astype(bf16)
        for load in value_loads:
            load.wait()
        for k, r in enumerate(portion):
            span = slice(8 * k, 8 * k + 8)
            stacked = jnp.concatenate([coarse[span].astype(f32), fine[span].astype(f32)], axis=0).astype(bf16)
            sums = jnp.dot(stacked, slots_ref[r, 1], preferred_element_type=f32)
            total = sums[:8] + sums[8:16] + own_weight[span] * fresh[r, 1:2]
            sums_ref[8 * r : 8 * r + 8] = total / mass[span]
    done = jnp.concatenate([sums_ref[pl.ds(g, count, stride=8), :] for g in range(group)], axis=1).astype(bf16)
    for k in range(out_ref.shape[0]):
        out_ref[k] = done
    leave.wait()


def resid_kernel(partial_ref, *refs):
    packs, out_ref = refs[:-1], refs[-1]
    count, width = partial_ref.shape[1:]
    columns = width // len(packs)
    back = lax.rem(len(packs) - lax.axis_index("x"), len(packs)) * columns
    total = partial_ref[0]
    for k in range(1, partial_ref.shape[0]):
        total = total + partial_ref[k]
    squares = jnp.zeros((count, 1), f32)
    blocks = []
    for step, pack_ref in enumerate(packs):
        tail = pack_ref[columns:].astype(f32)
        gain = (tail[count : count + 1] + tail[count + 1 : count + 2] + tail[count + 2 : count + 3])[:, :columns]
        hidden = pltpu.roll(tail[:count], back, 1)[:, :columns]
        resid = total[:, step * columns : (step + 1) * columns] + hidden
        resid = resid.astype(bf16).astype(f32)
        squares = squares + jnp.sum(resid * resid, axis=1, keepdims=True)
        blocks.append(resid * gain)
    shift = lax.rem(lax.axis_index("x") + 1, len(packs)) * columns
    ordered = pltpu.roll(jnp.concatenate(blocks[::-1], axis=1), shift, 1)
    lane = lax.broadcasted_iota(jnp.int32, (count, LANES), 1)
    spare = jnp.zeros((count, LANES), f32)
    for k, part in enumerate(three_parts(squares)):
        spare = jnp.where(lane == k, part, spare)
    done = jnp.concatenate([ordered, spare], axis=1).astype(bf16)
    for k in range(out_ref.shape[0]):
        out_ref[k] = done


def norm_kernel(rows_ref, out_ref):
    blocks, count, padded = rows_ref.shape
    width = padded - LANES
    squares = jnp.zeros((count, LANES), f32)
    for k in range(blocks):
        squares = squares + rows_ref[k, :, width:].astype(f32)
    factor = lax.rsqrt(jnp.sum(squares, axis=1, keepdims=True) / D + epsilon)
    for k in range(blocks):
        done = (rows_ref[k, :, :width].astype(f32) * factor).astype(bf16)
        for copy in range(out_ref.shape[0]):
            out_ref[copy, :, k * width : (k + 1) * width] = done


def fetch_kernel(head_hbm, after_ref, head_ref, sem):
    load = pltpu.make_async_copy(head_hbm, head_ref, sem)
    load.start()
    load.wait()


def logits_kernel(head_ref, rows_ref, ids_ref, logits_ref, stats_ref):
    depth = head_ref.shape[1]
    for k in range(depth // CHUNK):
        span = slice(k * CHUNK, (k + 1) * CHUNK)
        product = lax.dot_general(
            head_ref[:, span], rows_ref[:, span], (((1,), (1,)), ((), ())), preferred_element_type=f32
        )
        if k == 0:
            logits_ref[...] = product
        else:
            logits_ref[...] += product
    logits = logits_ref[...]
    top = jnp.max(logits, axis=0, keepdims=True)
    log_mass = top + jnp.log(jnp.sum(jnp.exp(logits - top), axis=0, keepdims=True))
    hits = lax.broadcasted_iota(jnp.int32, logits.shape, 0) == ids_ref[...]
    picked = jnp.sum(jnp.where(hits, logits, 0.0), axis=0, keepdims=True)
    stats_ref[...] = jnp.concatenate([log_mass, picked], axis=0)


def final_kernel(logits_ref, stats_ref, mu_ref, logprobs_ref, surprise_ref, mu_next_ref):
    masses = stats_ref[:, 0]
    top = jnp.max(masses, axis=0, keepdims=True)
    log_mass = top + jnp.log(jnp.sum(jnp.exp(masses - top), axis=0, keepdims=True))
    picked = jnp.sum(stats_ref[:, 1], axis=0, keepdims=True)
    logprobs_ref[...] = logits_ref[...] - log_mass
    surprise = (log_mass - picked) / math.log(2.0)
    surprise_ref[...] = surprise
    mu_next_ref[...] = mu_ref[...] - learn_rate * (surprise - target_bits)


def spread(block, axes, count):
    many = jnp.broadcast_to(block[None], (count,) + block.shape)
    return lax.all_to_all(many, axes, split_axis=0, concat_axis=0, tiled=False)


def shards(query, cache, new_kv, lengths, hidden_in, out_proj, final_gain, lm_head, tokens, mu):
    nz, nx, ny, nc = (lax.axis_size(a) for a in ("z", "x", "y", "c"))
    z, x, y, c = (lax.axis_index(a) for a in ("z", "x", "y", "c"))
    count = query.shape[0]
    heads, columns = out_proj.shape
    sizes = {"z": nz, "x": nx, "y": ny, "c": nc}

    def from_along_x(block, step):
        return lax.ppermute(block, "x", [(i, (i + step) % nx) for i in range(nx)])

    many, pack = pl.pallas_call(
        functools.partial(attend_kernel, HEADS // KV_HEADS, sizes),
        out_shape=[
            jax.ShapeDtypeStruct((nz,) + query.shape, bf16),
            jax.ShapeDtypeStruct((columns + TAIL, heads), bf16),
        ],
        in_specs=[IN_SMEM] + [IN_PLACE] * 6,
        out_specs=[IN_VMEM, IN_PLACE],
        scratch_shapes=[
            pltpu.VMEM(cache.shape, bf16),
            pltpu.VMEM((count * 8, HEAD_DIM), f32),
            pltpu.VMEM((count * 8, HEAD_DIM), f32),
            pltpu.VMEM(query.shape, bf16),
            pltpu.VMEM(new_kv.shape, bf16),
            pltpu.VMEM((columns, hidden_in.shape[0]), bf16),
            pltpu.VMEM((1, columns), f32),
            pltpu.VMEM((columns + TAIL, heads), bf16),
            pltpu.SemaphoreType.DMA((2, count)),
            pltpu.SemaphoreType.DMA((6,)),
        ],
        compiler_params=WHOLE,
        name="attend",
    )(lengths, query, new_kv, cache, out_proj.T, hidden_in.T, final_gain[None])
    packs = [pack] + [from_along_x(pack, k) for k in range(1, nx)]
    table = jnp.concatenate([out_proj.T] + [p[:columns] for p in packs[1:]], axis=0)
    gathered = lax.all_to_all(many, "z", split_axis=0, concat_axis=0, tiled=False)
    gathered = gathered.reshape(nz * count, -1)
    partial = lax.dot_general(
        gathered, table, (((1,), (1,)), ((), ())), preferred_element_type=f32
    )
    partial = partial.reshape(nz, count, nx * columns)
    partial = lax.all_to_all(partial, ("c", "y"), split_axis=0, concat_axis=0, tiled=False)

    width = nx * columns
    rows = pl.pallas_call(
        resid_kernel,
        out_shape=jax.ShapeDtypeStruct((nz, count, width + LANES), bf16),
        in_specs=[IN_VMEM] * (nx + 1),
        out_specs=IN_VMEM,
        compiler_params=SMALL,
        name="resid",
    )(partial, *packs)
    rows = lax.all_to_all(rows, "z", split_axis=0, concat_axis=0, tiled=False)
    half = pl.pallas_call(
        norm_kernel,
        out_shape=jax.ShapeDtypeStruct((nx * ny, count, nz * width), bf16),
        in_specs=[IN_VMEM],
        out_specs=IN_VMEM,
        compiler_params=SMALL,
        name="norm",
    )(rows)
    half = lax.all_to_all(half, ("y", "x"), split_axis=0, concat_axis=0, tiled=False)
    half = half.reshape(ny * nx * count, -1)
    other = lax.ppermute(half, "c", [(i, 1 - i) for i in range(2)])
    head = pl.pallas_call(
        fetch_kernel,
        out_shape=jax.ShapeDtypeStruct(lm_head.shape, bf16),
        in_specs=[IN_PLACE] * 2,
        out_specs=IN_VMEM,
        scratch_shapes=[pltpu.SemaphoreType.DMA],
        compiler_params=WIDE,
        name="fetch",
    )(lm_head, half)
    other, head = lax.optimization_barrier((other, head))
    first = jnp.where(c == 0, half, other)
    second = jnp.where(c == 0, other, half)
    everyone = jnp.concatenate([first, second], axis=0)

    vocab = lm_head.shape[0]
    requests = everyone.shape[0]
    offset = (((z * nx + x) * ny + y) * nc + c) * vocab
    logits, stats = pl.pallas_call(
        logits_kernel,
        out_shape=[jax.ShapeDtypeStruct((vocab, requests), f32), jax.ShapeDtypeStruct((2, requests), f32)],
        in_specs=[IN_VMEM] * 3,
        out_specs=[IN_VMEM] * 2,
        compiler_params=SMALL,
        name="logits",
    )(head, everyone, (tokens - offset)[None])

    stats = spread(stats, ("x", "y", "c"), nx * ny * nc)
    top = jnp.max(stats[:, 0], axis=0)
    log_mass = top + jnp.log(jnp.sum(jnp.exp(stats[:, 0] - top[None, :]), axis=0))
    picked = jnp.sum(stats[:, 1], axis=0)
    stats = spread(jnp.stack([log_mass, picked]), "z", nz)
    row_shape = jax.ShapeDtypeStruct((1, requests), f32)
    logprobs, surprise, mu_next = pl.pallas_call(
        final_kernel,
        out_shape=[jax.ShapeDtypeStruct((vocab, requests), f32), row_shape, row_shape],
        in_specs=[IN_VMEM] * 3,
        out_specs=[IN_VMEM] * 3,
        compiler_params=SMALL,
        name="final",
    )(logits, stats, mu[None])
    return (logprobs.T, surprise[0], mu_next[0])


def solution(mesh):
    grid = Mesh(np.asarray(mesh.devices).reshape(8, 4, 4, 2), ("z", "x", "y", "c"))
    dp, tensor = ("z", "x"), ("y", "c")
    placed = (
        P(dp, tensor),
        P(dp, None, None, tensor),
        P(dp, None, tensor),
        P(),
        P(None, dp),
        P(tensor, dp),
        P(dp),
        P(dp + tensor, None),
        P(),
        P(),
    )
    return jax.shard_map(
        shards,
        mesh=grid,
        in_specs=placed,
        out_specs=(P(None, dp + tensor), P(), P()),
        check_vma=False,
    )
```

```python
import functools
import math

import jax
import jax.numpy as jnp
import numpy as np
from jax import lax
from jax.experimental import pallas as pl
from jax.experimental.pallas import tpu as pltpu
from jax.sharding import Mesh
from jax.sharding import PartitionSpec as P

D = 5120
HEADS = 40
KV_HEADS = 8
HEAD_DIM = 128

masked_score = -1e30
epsilon = 1e-06
learn_rate = 0.1
target_bits = 5.0

bf16 = jnp.bfloat16
f32 = jnp.float32
LANES = 128

IN_VMEM = pl.BlockSpec(memory_space=pltpu.VMEM)
IN_SMEM = pl.BlockSpec(memory_space=pltpu.SMEM)
IN_PLACE = pl.BlockSpec(memory_space=pl.ANY)
SMALL = pltpu.CompilerParams(vmem_limit_bytes=20 << 20)
WIDE = pltpu.CompilerParams(vmem_limit_bytes=44 << 20)
WHOLE = pltpu.CompilerParams(vmem_limit_bytes=60 << 20)
TAIL = 16
CHUNK = 1280


def three_parts(wide):
    first = wide.astype(bf16).astype(f32)
    rest = wide - first
    second = rest.astype(bf16).astype(f32)
    third = (rest - second).astype(bf16).astype(f32)
    return first, second, third


def side_by_side(rows):
    return jnp.concatenate([rows[k : k + 8] for k in range(0, rows.shape[0], 8)], axis=1)


def pack_tail(sizes, hidden_ref, gain_ref, pack_ref):
    columns, requests = hidden_ref.shape
    heads = pack_ref.shape[1]
    rows = heads // columns * 8
    part = lax.axis_index("c") * sizes["y"] + lax.axis_index("y")
    row = lax.broadcasted_iota(jnp.int32, (rows, requests), 0)
    lane = lax.broadcasted_iota(jnp.int32, (rows, requests), 1)
    chosen = jnp.where(lane == row + part * rows, 1.0, 0.0).astype(bf16)
    picked = lax.dot_general(
        chosen, hidden_ref[...], (((1,), (1,)), ((), ())), preferred_element_type=f32
    )
    below = jnp.concatenate(three_parts(gain_ref[...]) + (jnp.zeros((5, columns), f32),), axis=0)
    below = jnp.concatenate([below, jnp.zeros((8, heads - columns), f32)], axis=1)
    pack_ref[columns:] = jnp.concatenate([side_by_side(picked), below], axis=0).astype(bf16)


def attend_kernel(group, sizes, lengths_ref, query_hbm, new_hbm, cache_ref, table_hbm, hidden_hbm, gain_hbm, *refs):
    out_ref, pack_hbm, slots_ref, rows_ref, sums_ref, query_ref, new_ref, hidden_ref, gain_ref, pack_ref = refs[:-2]
    sems, small_sems = refs[-2:]
    count, _, slots, head_dim = cache_ref.shape
    columns = table_hbm.shape[0]
    z, x = lax.axis_index("z"), lax.axis_index("x")
    scale = head_dim ** (-0.5)
    small = [
        pltpu.make_async_copy(source, target, small_sems.at[k])
        for k, (source, target) in enumerate(
            (
                (query_hbm, query_ref),
                (new_hbm, new_ref),
                (hidden_hbm, hidden_ref),
                (gain_hbm, gain_ref),
                (table_hbm, pack_ref.at[pl.ds(0, columns)]),
            )
        )
    ]
    leave = pltpu.make_async_copy(pack_ref, pack_hbm, small_sems.at[len(small)])
    portions = [range(k, k + count // 2) for k in (0, count // 2)]
    loads = [
        [
            pltpu.make_async_copy(cache_ref.at[r, kind], slots_ref.at[r, kind], sems.at[kind, r])
            for r in portion
        ]
        for portion in portions
        for kind in range(2)
    ]
    for load in small + sum(loads, []):
        load.start()
    for load in small[:2]:
        load.wait()

    query = query_ref[...].astype(f32)
    fresh = new_ref[...].astype(f32)
    rows_ref[...] = jnp.zeros_like(rows_ref)
    for g in range(group):
        rows_ref[pl.ds(g, count, stride=8), :] = query[:, g * head_dim : (g + 1) * head_dim]
    heads = rows_ref[...]
    new_keys = jnp.concatenate([jnp.broadcast_to(fresh[r, 0:1], (8, head_dim)) for r in range(count)], axis=0)
    own_scores = jnp.sum(heads * new_keys, axis=1, keepdims=True) * scale
    heads = heads.astype(bf16)
    position = lax.broadcasted_iota(jnp.int32, (8, slots), 1)
    base = (z * sizes["x"] + x) * count
    for portion, key_loads, value_loads in zip(portions, loads[::2], loads[1::2]):
        for load in key_loads:
            load.wait()
        scores = []
        for r in portion:
            score = lax.dot_general(
                heads[8 * r : 8 * r + 8],
                slots_ref[r, 0],
                (((1,), (1,)), ((), ())),
                preferred_element_type=f32,
            )
            scores.append(jnp.where(position < lengths_ref[base + r], score * scale, masked_score))
        scores = jnp.concatenate(scores, axis=0)
        own_score = own_scores[8 * portion[0] : 8 * portion[0] + scores.shape[0]]
        top = jnp.maximum(jnp.max(scores, axis=1, keepdims=True), own_score)
        weights = jnp.exp(scores - top)
        own_weight = jnp.exp(own_score - top)
        mass = jnp.sum(weights, axis=1, keepdims=True) + own_weight
        coarse = weights.astype(bf16)
        fine = (weights - coarse.astype(f32)).astype(bf16)
        if portion is portions[0]:
            for load in small[2:]:
                load.wait()
            pack_tail(sizes, hidden_ref, gain_ref, pack_ref)
            leave.start()
        for load in value_loads:
            load.wait()
        for k, r in enumerate(portion):
            span = slice(8 * k, 8 * k + 8)
            stacked = jnp.concatenate([coarse[span].astype(f32), fine[span].astype(f32)], axis=0).astype(bf16)
            sums = jnp.dot(stacked, slots_ref[r, 1], preferred_element_type=f32)
            total = sums[:8] + sums[8:16] + own_weight[span] * fresh[r, 1:2]
            sums_ref[8 * r : 8 * r + 8] = total / mass[span]
    done = jnp.concatenate([sums_ref[pl.ds(g, count, stride=8), :] for g in range(group)], axis=1).astype(bf16)
    for k in range(out_ref.shape[0]):
        out_ref[k] = done
    leave.wait()


def resid_kernel(partial_ref, *refs):
    packs, out_ref = refs[:-1], refs[-1]
    count, width = partial_ref.shape[1:]
    columns = width // len(packs)
    back = lax.rem(len(packs) - lax.axis_index("x"), len(packs)) * columns
    total = partial_ref[0]
    for k in range(1, partial_ref.shape[0]):
        total = total + partial_ref[k]
    squares = jnp.zeros((count, 1), f32)
    blocks = []
    for step, pack_ref in enumerate(packs):
        tail = pack_ref[columns:].astype(f32)
        gain = (tail[count : count + 1] + tail[count + 1 : count + 2] + tail[count + 2 : count + 3])[:, :columns]
        hidden = pltpu.roll(tail[:count], back, 1)[:, :columns]
        resid = total[:, step * columns : (step + 1) * columns] + hidden
        resid = resid.astype(bf16).astype(f32)
        squares = squares + jnp.sum(resid * resid, axis=1, keepdims=True)
        blocks.append(resid * gain)
    shift = lax.rem(lax.axis_index("x") + 1, len(packs)) * columns
    ordered = pltpu.roll(jnp.concatenate(blocks[::-1], axis=1), shift, 1)
    lane = lax.broadcasted_iota(jnp.int32, (count, LANES), 1)
    spare = jnp.zeros((count, LANES), f32)
    for k, part in enumerate(three_parts(squares)):
        spare = jnp.where(lane == k, part, spare)
    done = jnp.concatenate([ordered, spare], axis=1).astype(bf16)
    for k in range(out_ref.shape[0]):
        out_ref[k] = done


def norm_kernel(rows_ref, out_ref):
    blocks, count, padded = rows_ref.shape
    width = padded - LANES
    squares = jnp.zeros((count, LANES), f32)
    for k in range(blocks):
        squares = squares + rows_ref[k, :, width:].astype(f32)
    factor = lax.rsqrt(jnp.sum(squares, axis=1, keepdims=True) / D + epsilon)
    for k in range(blocks):
        done = (rows_ref[k, :, :width].astype(f32) * factor).astype(bf16)
        for copy in range(out_ref.shape[0]):
            out_ref[copy, :, k * width : (k + 1) * width] = done


def fetch_kernel(head_hbm, after_ref, head_ref, sem):
    load = pltpu.make_async_copy(head_hbm, head_ref, sem)
    load.start()
    load.wait()


def logits_kernel(head_ref, rows_ref, ids_ref, logits_ref, stats_ref):
    depth = head_ref.shape[1]
    for k in range(depth // CHUNK):
        span = slice(k * CHUNK, (k + 1) * CHUNK)
        product = lax.dot_general(
            head_ref[:, span], rows_ref[:, span], (((1,), (1,)), ((), ())), preferred_element_type=f32
        )
        if k == 0:
            logits_ref[...] = product
        else:
            logits_ref[...] += product
    logits = logits_ref[...]
    top = jnp.max(logits, axis=0, keepdims=True)
    log_mass = top + jnp.log(jnp.sum(jnp.exp(logits - top), axis=0, keepdims=True))
    hits = lax.broadcasted_iota(jnp.int32, logits.shape, 0) == ids_ref[...]
    picked = jnp.sum(jnp.where(hits, logits, 0.0), axis=0, keepdims=True)
    stats_ref[...] = jnp.concatenate([log_mass, picked], axis=0)


def final_kernel(logits_ref, stats_ref, mu_ref, logprobs_ref, surprise_ref, mu_next_ref):
    masses = stats_ref[:, 0]
    top = jnp.max(masses, axis=0, keepdims=True)
    log_mass = top + jnp.log(jnp.sum(jnp.exp(masses - top), axis=0, keepdims=True))
    picked = jnp.sum(stats_ref[:, 1], axis=0, keepdims=True)
    logprobs_ref[...] = logits_ref[...] - log_mass
    surprise = (log_mass - picked) / math.log(2.0)
    surprise_ref[...] = surprise
    mu_next_ref[...] = mu_ref[...] - learn_rate * (surprise - target_bits)


def spread(block, axes, count):
    many = jnp.broadcast_to(block[None], (count,) + block.shape)
    return lax.all_to_all(many, axes, split_axis=0, concat_axis=0, tiled=False)


def shards(query, cache, new_kv, lengths, hidden_in, out_proj, final_gain, lm_head, tokens, mu):
    nz, nx, ny, nc = (lax.axis_size(a) for a in ("z", "x", "y", "c"))
    z, x, y, c = (lax.axis_index(a) for a in ("z", "x", "y", "c"))
    count = query.shape[0]
    heads, columns = out_proj.shape
    sizes = {"z": nz, "x": nx, "y": ny, "c": nc}

    def from_along_x(block, step):
        return lax.ppermute(block, "x", [(i, (i + step) % nx) for i in range(nx)])

    many, pack = pl.pallas_call(
        functools.partial(attend_kernel, HEADS // KV_HEADS, sizes),
        out_shape=[
            jax.ShapeDtypeStruct((nz,) + query.shape, bf16),
            jax.ShapeDtypeStruct((columns + TAIL, heads), bf16),
        ],
        in_specs=[IN_SMEM] + [IN_PLACE] * 6,
        out_specs=[IN_VMEM, IN_PLACE],
        scratch_shapes=[
            pltpu.VMEM(cache.shape, bf16),
            pltpu.VMEM((count * 8, HEAD_DIM), f32),
            pltpu.VMEM((count * 8, HEAD_DIM), f32),
            pltpu.VMEM(query.shape, bf16),
            pltpu.VMEM(new_kv.shape, bf16),
            pltpu.VMEM((columns, hidden_in.shape[0]), bf16),
            pltpu.VMEM((1, columns), f32),
            pltpu.VMEM((columns + TAIL, heads), bf16),
            pltpu.SemaphoreType.DMA((2, count)),
            pltpu.SemaphoreType.DMA((6,)),
        ],
        compiler_params=WHOLE,
        name="attend",
    )(lengths, query, new_kv, cache, out_proj.T, hidden_in.T, final_gain[None])
    packs = [pack] + [from_along_x(pack, k) for k in range(1, nx)]
    table = jnp.concatenate([out_proj.T] + [p[:columns] for p in packs[1:]], axis=0)
    gathered = lax.all_to_all(many, "z", split_axis=0, concat_axis=0, tiled=False)
    gathered = gathered.reshape(nz * count, -1)
    partial = lax.dot_general(
        gathered, table, (((1,), (1,)), ((), ())), preferred_element_type=f32
    )
    partial = partial.reshape(nz, count, nx * columns)
    partial = lax.all_to_all(partial, ("c", "y"), split_axis=0, concat_axis=0, tiled=False)

    width = nx * columns
    rows = pl.pallas_call(
        resid_kernel,
        out_shape=jax.ShapeDtypeStruct((nz, count, width + LANES), bf16),
        in_specs=[IN_VMEM] * (nx + 1),
        out_specs=IN_VMEM,
        compiler_params=SMALL,
        name="resid",
    )(partial, *packs)
    rows = lax.all_to_all(rows, "z", split_axis=0, concat_axis=0, tiled=False)
    half = pl.pallas_call(
        norm_kernel,
        out_shape=jax.ShapeDtypeStruct((nx * ny, count, nz * width), bf16),
        in_specs=[IN_VMEM],
        out_specs=IN_VMEM,
        compiler_params=SMALL,
        name="norm",
    )(rows)
    half = lax.all_to_all(half, ("y", "x"), split_axis=0, concat_axis=0, tiled=False)
    half = half.reshape(ny * nx * count, -1)
    other = lax.ppermute(half, "c", [(i, 1 - i) for i in range(2)])
    head = pl.pallas_call(
        fetch_kernel,
        out_shape=jax.ShapeDtypeStruct(lm_head.shape, bf16),
        in_specs=[IN_PLACE] * 2,
        out_specs=IN_VMEM,
        scratch_shapes=[pltpu.SemaphoreType.DMA],
        compiler_params=WIDE,
        name="fetch",
    )(lm_head, half)
    other, head = lax.optimization_barrier((other, head))
    first = jnp.where(c == 0, half, other)
    second = jnp.where(c == 0, other, half)
    everyone = jnp.concatenate([first, second], axis=0)

    vocab = lm_head.shape[0]
    requests = everyone.shape[0]
    offset = (((z * nx + x) * ny + y) * nc + c) * vocab
    logits, stats = pl.pallas_call(
        logits_kernel,
        out_shape=[jax.ShapeDtypeStruct((vocab, requests), f32), jax.ShapeDtypeStruct((2, requests), f32)],
        in_specs=[IN_VMEM] * 3,
        out_specs=[IN_VMEM] * 2,
        compiler_params=SMALL,
        name="logits",
    )(head, everyone, (tokens - offset)[None])

    stats = spread(stats, ("x", "y", "c"), nx * ny * nc)
    top = jnp.max(stats[:, 0], axis=0)
    log_mass = top + jnp.log(jnp.sum(jnp.exp(stats[:, 0] - top[None, :]), axis=0))
    picked = jnp.sum(stats[:, 1], axis=0)
    stats = spread(jnp.stack([log_mass, picked]), "z", nz)
    row_shape = jax.ShapeDtypeStruct((1, requests), f32)
    logprobs, surprise, mu_next = pl.pallas_call(
        final_kernel,
        out_shape=[jax.ShapeDtypeStruct((vocab, requests), f32), row_shape, row_shape],
        in_specs=[IN_VMEM] * 3,
        out_specs=[IN_VMEM] * 3,
        compiler_params=SMALL,
        name="final",
    )(logits, stats, mu[None])
    return (logprobs.T, surprise[0], mu_next[0])


def solution(mesh):
    grid = Mesh(np.asarray(mesh.devices).reshape(8, 4, 4, 2), ("z", "x", "y", "c"))
    dp, tensor = ("z", "x"), ("y", "c")
    placed = (
        P(dp, tensor),
        P(dp, None, None, tensor),
        P(dp, None, tensor),
        P(),
        P(None, dp),
        P(tensor, dp),
        P(dp),
        P(dp + tensor, None),
        P(),
        P(),
    )
    return jax.shard_map(
        shards,
        mesh=grid,
        in_specs=placed,
        out_specs=(P(None, dp + tensor), P(), P()),
        check_vma=False,
    )
```
